512 devices in a mesh: rep: 64 (over y_hi, z, x), tp: 8 (over y_lo, core).
Axes of the slice: x: 4, y: 8 (y_hi: 2, y_lo: 4; y = y_hi * 4 + y_lo), z: 8, core: 2. Of those that a mesh axis runs over, the one named last changes fastest.
Arguments:
- tokens: bfloat16 [24576, 12288], P('rep', 'tp'), may hold values from -6 to 6
- tenant: int32 [24576], P('rep'), may hold values from 0 to 2
- offsets: int32 [64], P('rep'), may hold values from 0 to 4095
- store_index: int32 [1], replicated, may hold values from 0 to 63
- frozen_key_weight: bfloat16 [12288, 1024], P('tp'), may hold values from -0.0546875 to 0.0546875
- store_a: float32 [64, 64, 12288], P('rep', None, 'tp'), may hold values from -0.0546875 to 0.0546875
- store_b: float32 [64, 1024, 64], P('rep', 'tp'), may hold values from -0.36 to 0.36
- bank_a: bfloat16 [64, 12288], P(None, 'tp'), may hold values from -0.0546875 to 0.0546875
- bank_b: bfloat16 [1024, 64], P('tp'), may hold values from -0.359375 to 0.359375
Outputs:
- key_rows: bfloat16 [24576, 1024], P('rep', 'tp')
The draws below stay inside these ranges and needn't reach their ends.
Inputs may be any that keep to these rules, and one draw needn't show every extreme that they name: 0 marks a tenant without adapter, 1 the tenant of bank_a and bank_b, 2 the tenant whose adapter is merged.
All inputs are finite; a program needn't handle non-finite values.
Results may differ from the reference program's by a relative error of at most 0.0085.
Values may be sent and summed in bfloat16 or wider, within the bound.
A program may use at most 64 MiB of HBM per device.

```python
import math
import jax
import jax.numpy as jnp
from jax import lax

D = 12288
KV_HEADS = 8
HEAD = 128
RANK = 64
TOK_DEV = 384
KV = 1024
TOKENS = 24576
N_REP = 64


def with_ends(drawn, stream_key, low, top_value):
    longest = drawn.shape.index(max(drawn.shape))
    spots = []
    for shift in (0, 1):
        where = [jax.random.randint(jax.random.fold_in(stream_key, axis), (), 0, length) for axis, length in enumerate(drawn.shape)]
        where[longest] = (where[longest] + shift) % drawn.shape[longest]
        spots.append(tuple(where))
    return drawn.at[spots[0]].set(low).at[spots[1]].set(top_value)


def steps_of(key, dims, cuts, low, high):
    loudness = 1.0
    for dim, blocks in cuts:
        draws = jax.random.uniform(jax.random.fold_in(jax.random.fold_in(key, 6), dim), (blocks,), jnp.float32, low / len(cuts), high / len(cuts))
        loudness = loudness * jnp.repeat(jnp.exp(draws), dims[dim] // blocks).reshape((-1,) + (1,) * (len(dims) - 1 - dim))
    return loudness


def centred(rng, dims, width, reach, cuts=(), held_as=jnp.bfloat16):
    drawn = width * jax.random.normal(rng, dims, jnp.float32)
    if cuts:
        drawn = drawn * steps_of(rng, dims, cuts, -0.22, 0.18)
    return jnp.clip(drawn, -reach, reach).astype(held_as)


def setup_inputs(seed: int = 0) -> dict:
    keys = jax.random.split(jax.random.key(seed), 10)
    tokens = centred(keys[0], (TOKENS, D), 1.0, 6.0, ((0, 64), (1, 8)))
    tenant = with_ends(jax.random.randint(keys[1], (TOKENS,), 0, 3), jax.random.fold_in(keys[1], 1), 0, 2).astype(jnp.int32)
    offsets = with_ends(jax.random.randint(keys[2], (N_REP,), 0, 4096), jax.random.fold_in(keys[2], 1), 0, 4095).astype(jnp.int32)
    store_index = jax.random.randint(keys[3], (1,), 0, N_REP).astype(jnp.int32)
    frozen_key_weight = centred(keys[4], (D, KV), D ** -0.5, 0.0546875, ((0, 8),))
    store_a = centred(keys[5], (N_REP, RANK, D), D ** -0.5, 0.0546875, ((0, 64), (2, 8)), jnp.float32)
    store_b = centred(keys[6], (N_REP, KV, RANK), 0.06, 0.36, ((0, 64), (1, 8)), jnp.float32)
    bank_a = centred(keys[7], (RANK, D), D ** -0.5, 0.0546875, ((1, 8),))
    bank_b = centred(keys[8], (KV, RANK), 0.06, 0.359375, ((0, 8),))
    return dict(tokens=tokens, tenant=tenant, offsets=offsets, store_index=store_index, frozen_key_weight=frozen_key_weight, store_a=store_a, store_b=store_b, bank_a=bank_a, bank_b=bank_b)


adapter_scale = 2.0


def rotate(heads, positions):
    half_width = heads.shape[-1] // 2
    inv_freq = jnp.exp(jnp.arange(half_width, dtype=jnp.float32) * (-2.0 * math.log(1e6) / heads.shape[-1]))
    angles = positions.astype(jnp.float32)[:, None] * inv_freq[None, :]
    cosine = jnp.cos(angles)[:, None, :]
    sine_vals = jnp.sin(angles)[:, None, :]
    leading = heads[..., :half_width]
    trailing = heads[..., half_width:]
    return jnp.concatenate([leading * cosine - trailing * sine_vals, trailing * cosine + leading * sine_vals], axis=-1)


def reference(tokens, tenant, offsets, store_index, frozen_key_weight, store_a, store_b, bank_a, bank_b):
    root_index = store_index[0]
    factor_a = lax.dynamic_index_in_dim(store_a, root_index, 0, keepdims=False)
    factor_b = lax.dynamic_index_in_dim(store_b, root_index, 0, keepdims=False)
    weight_update = jnp.dot(factor_a.T, factor_b.T, precision=lax.Precision.HIGHEST)
    merged_key_weight = (frozen_key_weight.astype(jnp.float32) + adapter_scale * weight_update).astype(jnp.bfloat16)
    is_new = (tenant == 2)[:, None]
    blank = jnp.zeros_like(tokens)
    new_rows = jnp.where(is_new, tokens, blank)
    old_rows = jnp.where(is_new, blank, tokens)
    projected_keys = jnp.dot(old_rows, frozen_key_weight, preferred_element_type=jnp.float32) + jnp.dot(new_rows, merged_key_weight, preferred_element_type=jnp.float32)
    shrink = jnp.dot(tokens, bank_a.T, preferred_element_type=jnp.float32)
    expand_factor = jnp.dot(shrink, bank_b.astype(jnp.float32).T, precision=lax.Precision.HIGHEST)
    adapted_keys = projected_keys + jnp.where((tenant == 1)[:, None], adapter_scale * expand_factor, jnp.float32(0.0))
    positions = (offsets[:, None] + jnp.arange(TOK_DEV, dtype=jnp.int32)[None, :]).reshape(-1)
    rotated = rotate(adapted_keys.reshape(TOKENS, KV_HEADS, HEAD), positions)
    return rotated.reshape(TOKENS, KV).astype(jnp.bfloat16)
```

```python
import functools
import math

import jax
import jax.numpy as jnp
from jax import lax
from jax.experimental import pallas as pl
from jax.experimental.pallas import tpu as pltpu
from jax.sharding import PartitionSpec as P

MESH = pl.DeviceIdType.MESH
SCALE = 2.0
NY, NZ, NX = 2, 8, 4
NT = 8
ROWS = 384
FEAT = 1536
HEAD = 128
RANK = 64
PART = ROWS // NT
TILES = 7
SLICE = 16 * TILES


def kernel(
    index_ref, offset_ref, tenant_ref, tok_hbm, w_hbm, a_hbm, bt_hbm, ba_hbm, bbt_hbm, out_ref,
    tok, w, a_raw, bt_raw, ranks, ups,
    z_src, z_got, x_got, y_got, g_got,
    part_src, part_got, low_src, low_got, low_sum,
    acc, cos2, sin2,
    load_sem, z_ss, z_rs, x_ss, x_rs, y_ss, y_rs, g_ss, g_rs, p_ss, p_rs, s_ss, s_rs, t_ss, t_rs,
):
    rep, t = lax.axis_index("rep"), lax.axis_index("tp")
    yh, z, x = rep // (NZ * NX), (rep // NX) % NZ, rep % NX

    def at(yh_, z_, x_):
        return (yh_ * NZ + z_) * NX + x_

    z_of = [(z + k) % NZ for k in range(1, NZ)]
    x_of = [(x + k) % NX for k in range(1, NX)]
    t_of = [(t + k) % NT for k in range(1, NT)]
    z_peers = [(at(yh, q, x), t) for q in z_of]
    x_peers = [(at(yh, z, q), t) for q in x_of]
    y_peer = (at(1 - yh, z, x), t)
    t_peers = [(rep, q) for q in t_of]

    barrier = pltpu.get_barrier_semaphore()
    peers = z_peers + x_peers + [y_peer] + t_peers
    for peer in peers:
        pl.semaphore_signal(barrier, inc=1, device_id=peer, device_id_type=MESH)

    loads = [
        pltpu.make_async_copy(src, dst, load_sem.at[i])
        for i, (src, dst) in enumerate(
            [
                (a_hbm, a_raw),
                (bt_hbm, bt_raw),
                (tok_hbm, tok),
                (w_hbm, w),
                (ba_hbm, ranks.at[pl.ds(0, RANK)]),
                (bbt_hbm, ups.at[pl.ds(0, RANK)]),
            ]
        )
    ]
    for load in loads:
        load.start()

    root = index_ref[0]
    root_y, root_z, root_x = root // (NZ * NX), (root // NX) % NZ, root % NX

    loads[0].wait()
    loads[1].wait()
    for q in range(NZ):
        block, half = q // 2, q % 2
        for j in range(TILES - 1):
            column = (half * (TILES - 1) + j) * HEAD
            z_src[q, 16 * j : 16 * (j + 1), :] = a_raw[
                16 * block : 16 * (block + 1), column : column + HEAD
            ].astype(jnp.bfloat16)
        z_src[q, 16 * (TILES - 1) :, :] = bt_raw[16 * block : 16 * (block + 1), :].astype(jnp.bfloat16)

    pl.semaphore_wait(barrier, len(peers))

    def send(src, dst, ss, rs, peer):
        copy = pltpu.make_async_remote_copy(
            src_ref=src, dst_ref=dst, send_sem=ss, recv_sem=rs, device_id=peer, device_id_type=MESH
        )
        copy.start()
        return copy

    sent = []
    z_copies = [
        send(z_src.at[z_of[i]], z_got.at[z], z_ss.at[i], z_rs.at[i], z_peers[i]) for i in range(NZ - 1)
    ]
    z_got[z] = z_src[z]

    loads[2].wait()
    loads[3].wait()
    p_copies = []
    for k in range(1, NT):
        q = t_of[k - 1]
        column = pl.multiple_of(q * HEAD, HEAD)
        part_src[k - 1] = jnp.dot(
            tok[...], w[:, pl.ds(column, HEAD)], preferred_element_type=jnp.float32
        ).astype(jnp.bfloat16)
        p_copies.append(
            send(part_src.at[k - 1], part_got.at[k - 1], p_ss.at[k - 1], p_rs.at[k - 1], t_peers[k - 1])
        )

    for copy in z_copies:
        copy.wait_recv()
    x_got[x] = z_got[root_z]
    x_copies = [
        send(x_got.at[x], x_got.at[x], x_ss.at[i], x_rs.at[i], x_peers[i]) for i in range(NX - 1)
    ]
    acc[...] = jnp.dot(
        tok[...],
        w[:, pl.ds(pl.multiple_of(t * HEAD, HEAD), HEAD)],
        preferred_element_type=jnp.float32,
    )
    for copy in x_copies:
        copy.wait_recv()
    y_got[yh] = x_got[root_x]
    y_copy = send(y_got.at[yh], y_got.at[yh], y_ss, y_rs, y_peer)

    lane = lax.broadcasted_iota(jnp.int32, (ROWS, HEAD), 1)
    row = lax.broadcasted_iota(jnp.int32, (ROWS, HEAD), 0)
    pair = (lane % (HEAD // 2)).astype(jnp.float32)
    freq = jnp.exp(pair * (-2.0 * math.log(1000000.0) / HEAD))
    angle = (offset_ref[0] + row).astype(jnp.float32) * freq
    cos2[...] = jnp.cos(angle)
    sine = jnp.sin(angle)
    sin2[...] = jnp.where(lane < HEAD // 2, -sine, sine)

    y_copy.wait_recv()
    g_got[z] = y_got[root_y]
    g_copies = [
        send(g_got.at[z], g_got.at[z], g_ss.at[i], g_rs.at[i], z_peers[i]) for i in range(NZ - 1)
    ]
    total = acc[...]
    for i, copy in enumerate(p_copies):
        copy.wait_recv()
        total = total + part_got[i].astype(jnp.float32)
    acc[...] = total
    loads[4].wait()
    loads[5].wait()

    eye = lax.broadcasted_iota(jnp.int32, (HEAD, HEAD), 0) == lax.broadcasted_iota(
        jnp.int32, (HEAD, HEAD), 1
    )
    columns = [
        jnp.sum(
            jnp.where(eye, tenant_ref[:, HEAD * i : HEAD * (i + 1)], 0).astype(jnp.float32),
            axis=1,
            keepdims=True,
        )
        for i in range(ROWS // HEAD)
    ]
    tenant = jnp.concatenate(columns, axis=0)
    wanted = jnp.where(lane < RANK, 1.0, 2.0)

    for copy in g_copies:
        copy.wait_recv()
    for q in range(NZ):
        block, half = q // 2, q % 2
        for j in range(TILES - 1):
            column = (half * (TILES - 1) + j) * HEAD
            ranks[RANK + 16 * block : RANK + 16 * (block + 1), column : column + HEAD] = g_got[
                q, 16 * j : 16 * (j + 1), :
            ]
        if half == 0:
            ups[RANK + 16 * block : RANK + 16 * (block + 1), :] = g_got[q, 16 * (TILES - 1) :, :]
    low = lax.dot_general(
        tok[...], ranks[...], (((1,), (1,)), ((), ())), preferred_element_type=jnp.float32
    )
    low_src[...] = jnp.where(tenant == wanted, low, 0.0).astype(jnp.bfloat16)

    def rows_of(q):
        return pl.ds(pl.multiple_of(q * PART, 16), PART)

    s_copies = [
        send(low_src.at[rows_of(t_of[i])], low_got.at[i], s_ss.at[i], s_rs.at[i], t_peers[i])
        for i in range(NT - 1)
    ]
    total = low_src[rows_of(t), :].astype(jnp.float32)
    for i, copy in enumerate(s_copies):
        copy.wait_recv()
        total = total + low_got[i].astype(jnp.float32)
    low_sum[rows_of(t), :] = total.astype(jnp.bfloat16)
    t_copies = [
        send(low_sum.at[rows_of(t)], low_sum.at[rows_of(t)], t_ss.at[i], t_rs.at[i], t_peers[i])
        for i in range(NT - 1)
    ]
    for copy in z_copies + p_copies + x_copies + [y_copy] + g_copies + s_copies:
        copy.wait_send()
    for copy in t_copies:
        copy.wait_recv()
    adapted = acc[...] + SCALE * jnp.dot(low_sum[...], ups[...], preferred_element_type=jnp.float32)
    swapped = pltpu.roll(adapted, HEAD // 2, 1)
    out_ref[...] = (adapted * cos2[...] + swapped * sin2[...]).astype(jnp.bfloat16)
    for copy in t_copies:
        copy.wait_send()


def per_device(
    tokens, tenant, offsets, store_index, frozen_key_weight, store_a, store_b, bank_a, bank_b
):
    bf16, f32 = jnp.bfloat16, jnp.float32
    smem = pl.BlockSpec(memory_space=pltpu.SMEM)
    vmem = pl.BlockSpec(memory_space=pltpu.VMEM)
    hbm = pl.BlockSpec(memory_space=pl.ANY)
    dma = pltpu.SemaphoreType.DMA
    return pl.pallas_call(
        kernel,
        out_shape=jax.ShapeDtypeStruct((ROWS, HEAD), bf16),
        in_specs=[smem, smem, vmem] + [hbm] * 6,
        out_specs=vmem,
        scratch_shapes=[
            pltpu.VMEM((ROWS, FEAT), bf16),
            pltpu.VMEM((FEAT, NT * HEAD), bf16),
            pltpu.VMEM((RANK, FEAT), f32),
            pltpu.VMEM((RANK, HEAD), f32),
            pltpu.VMEM((2 * RANK, FEAT), bf16),
            pltpu.VMEM((2 * RANK, HEAD), bf16),
            pltpu.VMEM((NZ, SLICE, HEAD), bf16),
            pltpu.VMEM((NZ, SLICE, HEAD), bf16),
            pltpu.VMEM((NX, SLICE, HEAD), bf16),
            pltpu.VMEM((NY, SLICE, HEAD), bf16),
            pltpu.VMEM((NZ, SLICE, HEAD), bf16),
            pltpu.VMEM((NT - 1, ROWS, HEAD), bf16),
            pltpu.VMEM((NT - 1, ROWS, HEAD), bf16),
            pltpu.VMEM((ROWS, 2 * RANK), bf16),
            pltpu.VMEM((NT - 1, PART, 2 * RANK), bf16),
            pltpu.VMEM((ROWS, 2 * RANK), bf16),
            pltpu.VMEM((ROWS, HEAD), f32),
            pltpu.VMEM((ROWS, HEAD), f32),
            pltpu.VMEM((ROWS, HEAD), f32),
            dma((6,)),
            dma((NZ - 1,)), dma((NZ - 1,)),
            dma((NX - 1,)), dma((NX - 1,)),
            dma, dma,
            dma((NZ - 1,)), dma((NZ - 1,)),
            dma((NT - 1,)), dma((NT - 1,)),
            dma((NT - 1,)), dma((NT - 1,)),
            dma((NT - 1,)), dma((NT - 1,)),
        ],
        compiler_params=pltpu.CompilerParams(
            collective_id=0, has_side_effects=True, vmem_limit_bytes=60 * 1024 * 1024
        ),
        name="key_rows",
    )(
        store_index,
        offsets,
        tenant.reshape(1, ROWS),
        tokens,
        frozen_key_weight,
        store_a[0],
        store_b[0].T,
        bank_a,
        bank_b.T,
    )


def solution(mesh):
    in_specs = (
        P("rep", "tp"),
        P("rep"),
        P("rep"),
        P(),
        P("tp", None),
        P("rep", None, "tp"),
        P("rep", "tp", None),
        P(None, "tp"),
        P("tp", None),
    )
    return jax.shard_map(
        per_device, mesh=mesh, in_specs=in_specs, out_specs=P("rep", "tp"), check_vma=False
    )
```

```python
import math

import jax
import jax.numpy as jnp
from jax import lax
from jax.experimental import pallas as pl
from jax.experimental.pallas import tpu as pltpu
from jax.sharding import PartitionSpec as P

MESH = pl.DeviceIdType.MESH
SCALE = 2.0
NY, NZ, NX = 2, 8, 4
NC = 4
ROWS = 384
FEAT = 1536
HEAD = 128
RANK = 64
HALF = ROWS // 2
PACK = ROWS // 4
TILES = (4, 3)
CHUNK = FEAT // 2


def kernel(
    index_ref, offset_ref, tenant_ref, tok_hbm, w_hbm, a_hbm, bt_hbm, ba_hbm, bbt_hbm, out_ref,
    tok, w, a_raw, bt_raw, bank, ranks, bank_up, up,
    z_src0, z_src1, z_got0, z_got1, x_got0, x_got1, y_got0, y_got1, g_got0, g_got1,
    mine, pair_src, pair_got, part_src, part_got,
    l_mine, l_src, l_got, l_chip, l_chips, l_all,
    acc, cos2, sin2,
    load_sem, z_ss, z_rs, x_ss, x_rs, y_ss, y_rs, g_ss, g_rs, q_ss, q_rs, p_ss, p_rs, l_ss, l_rs,
):
    bf16, f32 = jnp.bfloat16, jnp.float32
    rep, t = lax.axis_index("rep"), lax.axis_index("tp")
    yh, z, x = rep // (NZ * NX), (rep // NX) % NZ, rep % NX
    yl, core = t // 2, t % 2

    def at(yh_, z_, x_):
        return (yh_ * NZ + z_) * NX + x_

    z_of = [(z + k) % NZ for k in range(1, NZ)]
    x_of = [(x + k) % NX for k in range(1, NX)]
    c_of = [(yl + k) % NC for k in range(1, NC)]
    z_peers = [(at(yh, q, x), t) for q in z_of]
    x_peers = [(at(yh, z, q), t) for q in x_of]
    y_peer = (at(1 - yh, z, x), t)
    c_peers = [(rep, 2 * q + core) for q in c_of]
    twin = (rep, 2 * yl + 1 - core)

    barrier = pltpu.get_barrier_semaphore()
    peers = z_peers + x_peers + [y_peer] + c_peers + [twin]
    for peer in peers:
        pl.semaphore_signal(barrier, inc=1, device_id=peer, device_id_type=MESH)

    bank_up[...] = jnp.zeros_like(bank_up)
    up[...] = jnp.zeros_like(up)
    loads = [
        pltpu.make_async_copy(src, dst, load_sem.at[i])
        for i, (src, dst) in enumerate(
            [
                (a_hbm, a_raw),
                (bt_hbm, bt_raw),
                (tok_hbm, tok),
                (ba_hbm, bank.at[pl.ds(0, RANK)]),
                (ba_hbm, bank.at[pl.ds(RANK, RANK)]),
                (w_hbm, w),
                (bbt_hbm, bank_up.at[pl.ds(0, RANK), pl.ds(0, HEAD)]),
                (bbt_hbm, bank_up.at[pl.ds(RANK, RANK), pl.ds(HEAD, HEAD)]),
            ]
        )
    ]
    for load in loads:
        load.start()

    root = index_ref[0]
    root_y, root_z, root_x = root // (NZ * NX), (root // NX) % NZ, root % NX

    z_src, z_got, x_got, y_got, g_got = (
        (z_src0, z_src1), (z_got0, z_got1), (x_got0, x_got1), (y_got0, y_got1), (g_got0, g_got1)
    )

    def tile(q, chunk, j):
        return 16 * (q // 2), chunk * CHUNK + ((q % 2) * 3 + j) * HEAD

    loads[0].wait()
    loads[1].wait()
    for chunk in range(2):
        for q in range(NZ):
            for j in range(3):
                row, column = tile(q, chunk, j)
                z_src[chunk][q, 16 * j : 16 * (j + 1), :] = a_raw[
                    row : row + 16, column : column + HEAD
                ].astype(bf16)
            if chunk == 0:
                row = 16 * (q // 2)
                z_src[chunk][q, 48:64, :] = bt_raw[row : row + 16, :].astype(bf16)

    pl.semaphore_wait(barrier, len(peers))

    started = []

    def send(src, dst, ss, rs, peer):
        copy = pltpu.make_async_remote_copy(
            src_ref=src, dst_ref=dst, send_sem=ss, recv_sem=rs, device_id=peer, device_id_type=MESH
        )
        copy.start()
        started.append(copy)
        return copy

    def arrived(copies):
        for copy in copies:
            copy.wait_recv()

    z_copies = [
        [
            send(
                z_src[chunk].at[z_of[i]], z_got[chunk].at[z],
                z_ss.at[chunk, i], z_rs.at[chunk, i], z_peers[i],
            )
            for i in range(NZ - 1)
        ]
        for chunk in range(2)
    ]
    for chunk in range(2):
        z_got[chunk][z] = z_src[chunk][z]

    lane = lax.broadcasted_iota(jnp.int32, (PACK, HEAD), 1)
    left = lane < RANK

    def low_start(s, low):
        halves = [
            jnp.where(left, low[HALF * h : HALF * h + PACK], low[HALF * h + PACK : HALF * (h + 1)])
            for h in range(2)
        ]
        l_mine[s] = jnp.where(core == 0, halves[0], halves[1])
        l_src[s] = jnp.where(core == 0, halves[1], halves[0]).astype(bf16)
        return send(l_src.at[s], l_got.at[s], l_ss.at[s, 0], l_rs.at[s, 0], twin)

    def low_spread(s, copy):
        copy.wait_recv()
        l_chip[s] = (l_mine[s] + l_got[s].astype(f32)).astype(bf16)
        return [
            send(l_chip.at[s], l_chips.at[s, i], l_ss.at[s, 1 + i], l_rs.at[s, 1 + i], c_peers[i])
            for i in range(NC - 1)
        ]

    def low_join(s, copies):
        total = l_chip[s].astype(f32)
        for i, copy in enumerate(copies):
            copy.wait_recv()
            total = total + l_chips[s, i].astype(f32)
        l_all[s, core] = total.astype(bf16)
        return send(l_all.at[s, core], l_all.at[s, core], l_ss.at[s, NC], l_rs.at[s, NC], twin)

    def expanded(s, copy, ups):
        copy.wait_recv()
        parts = []
        for h in range(2):
            both = jnp.dot(l_all[s, h], ups[...], preferred_element_type=f32)
            parts += [both[:, :HEAD], both[:, HEAD:]]
        return SCALE * jnp.concatenate(parts, axis=0)

    def times_ranks(a, b):
        return lax.dot_general(a, b, (((1,), (1,)), ((), ())), preferred_element_type=f32)

    loads[2].wait()
    loads[3].wait()
    loads[4].wait()
    bank_step = low_start(0, times_ranks(tok[...], bank[...]))

    loads[5].wait()
    order = c_of + [yl]
    pair_copies = []
    part_copies = []

    def passed(k):
        pair_copies[k].wait_recv()
        total = mine[k] + pair_got[k].astype(f32)
        if k == NC - 1:
            acc[...] = total
            return
        part_src[k] = total.astype(bf16)
        part_copies.append(
            send(part_src.at[k], part_got.at[k], p_ss.at[k], p_rs.at[k], c_peers[k])
        )

    for k, q in enumerate(order):
        column = pl.multiple_of(q * 2 * HEAD, 2 * HEAD)
        both = jnp.dot(tok[...], w[:, pl.ds(column, 2 * HEAD)], preferred_element_type=f32)
        mine[k] = jnp.where(core == 0, both[:, :HEAD], both[:, HEAD:])
        pair_src[k] = jnp.where(core == 0, both[:, HEAD:], both[:, :HEAD]).astype(bf16)
        pair_copies.append(send(pair_src.at[k], pair_got.at[k], q_ss.at[k], q_rs.at[k], twin))
        if k == 1:
            bank_step = low_spread(0, bank_step)
        if k >= 1:
            passed(k - 1)
    passed(NC - 1)

    wide = lax.broadcasted_iota(jnp.int32, (HALF, HEAD), 1)
    row = lax.broadcasted_iota(jnp.int32, (HALF, HEAD), 0)
    row = jnp.where(wide < HEAD // 2, row, row + HALF)
    freq = jnp.exp((wide % (HEAD // 2)).astype(f32) * (-2.0 * math.log(1000000.0) / HEAD))
    angle = (offset_ref[0] + row).astype(f32) * freq
    first = wide < HEAD // 2
    cosine, sine = jnp.cos(angle), jnp.sin(angle)
    turned_cos, turned_sin = pltpu.roll(cosine, HEAD // 2, 1), pltpu.roll(sine, HEAD // 2, 1)
    cos2[0:HALF, :] = jnp.where(first, cosine, turned_cos)
    cos2[HALF:, :] = jnp.where(first, turned_cos, cosine)
    sin2[0:HALF, :] = jnp.where(first, -sine, turned_sin)
    sin2[HALF:, :] = jnp.where(first, -turned_sin, sine)

    x_copies, y_copies, g_copies = [], [], []
    for chunk in range(2):
        arrived(z_copies[chunk])
        x_got[chunk][x] = z_got[chunk][root_z]
        x_copies.append(
            [
                send(
                    x_got[chunk].at[x], x_got[chunk].at[x],
                    x_ss.at[chunk, i], x_rs.at[chunk, i], x_peers[i],
                )
                for i in range(NX - 1)
            ]
        )
    for chunk in range(2):
        arrived(x_copies[chunk])
        y_got[chunk][yh] = x_got[chunk][root_x]
        y_copies.append(
            send(y_got[chunk].at[yh], y_got[chunk].at[yh], y_ss.at[chunk], y_rs.at[chunk], y_peer)
        )
    bank_step = low_join(0, bank_step)

    eye = lax.broadcasted_iota(jnp.int32, (HEAD, HEAD), 0) == lax.broadcasted_iota(
        jnp.int32, (HEAD, HEAD), 1
    )
    tenant = jnp.concatenate(
        [
            jnp.sum(
                jnp.where(eye, tenant_ref[pl.ds(HEAD * i, HEAD)].reshape(1, HEAD), 0).astype(f32),
                axis=1,
                keepdims=True,
            )
            for i in range(ROWS // HEAD)
        ],
        axis=0,
    )

    for chunk in range(2):
        y_copies[chunk].wait_recv()
        g_got[chunk][z] = y_got[chunk][root_y]
        g_copies.append(
            [
                send(
                    g_got[chunk].at[z], g_got[chunk].at[z],
                    g_ss.at[chunk, i], g_rs.at[chunk, i], z_peers[i],
                )
                for i in range(NZ - 1)
            ]
        )

    total = acc[...]
    for k, copy in enumerate(part_copies):
        copy.wait_recv()
        total = total + part_got[k].astype(f32)
    loads[6].wait()
    loads[7].wait()
    acc[...] = total + jnp.where(tenant == 1.0, expanded(0, bank_step, bank_up), 0.0)

    low = None
    for chunk in range(2):
        arrived(g_copies[chunk])
        for q in range(NZ):
            for j in range(3):
                row, column = tile(q, chunk, j)
                value = g_got[chunk][q, 16 * j : 16 * (j + 1), :]
                ranks[row : row + 16, column : column + HEAD] = value
                ranks[RANK + row : RANK + row + 16, column : column + HEAD] = value
        columns = slice(chunk * CHUNK, (chunk + 1) * CHUNK)
        term = times_ranks(tok[:, columns], ranks[:, columns])
        low = term if low is None else low + term
    store_step = low_start(1, low)
    for q in range(0, NZ, 2):
        row = 16 * (q // 2)
        value = g_got[0][q, 48:64, :]
        up[row : row + 16, 0:HEAD] = value
        up[RANK + row : RANK + row + 16, HEAD:] = value
    store_step = low_spread(1, store_step)
    store_step = low_join(1, store_step)
    adapted = acc[...] + jnp.where(tenant == 2.0, expanded(1, store_step, up), 0.0)
    swapped = pltpu.roll(adapted, HEAD // 2, 1)
    out_ref[...] = (adapted * cos2[...] + swapped * sin2[...]).astype(bf16)
    for copy in started:
        copy.wait_send()


def per_device(
    tokens, tenant, offsets, store_index, frozen_key_weight, store_a, store_b, bank_a, bank_b
):
    bf16, f32 = jnp.bfloat16, jnp.float32
    smem = pl.BlockSpec(memory_space=pltpu.SMEM)
    vmem = pl.BlockSpec(memory_space=pltpu.VMEM)
    hbm = pl.BlockSpec(memory_space=pl.ANY)
    dma = pltpu.SemaphoreType.DMA

    def slices(n):
        return [pltpu.VMEM((n, 16 * tiles, HEAD), bf16) for tiles in TILES]

    return pl.pallas_call(
        kernel,
        out_shape=jax.ShapeDtypeStruct((ROWS, HEAD), bf16),
        in_specs=[smem, smem, vmem] + [hbm] * 6,
        out_specs=vmem,
        scratch_shapes=[
            pltpu.VMEM((ROWS, FEAT), bf16),
            pltpu.VMEM((FEAT, 2 * NC * HEAD), bf16),
            pltpu.VMEM((RANK, FEAT), f32),
            pltpu.VMEM((RANK, HEAD), f32),
            pltpu.VMEM((2 * RANK, FEAT), bf16),
            pltpu.VMEM((2 * RANK, FEAT), bf16),
            pltpu.VMEM((2 * RANK, 2 * HEAD), bf16),
            pltpu.VMEM((2 * RANK, 2 * HEAD), bf16),
            *slices(NZ), *slices(NZ), *slices(NX), *slices(NY), *slices(NZ),
            pltpu.VMEM((NC, ROWS, HEAD), f32),
            pltpu.VMEM((NC, ROWS, HEAD), bf16),
            pltpu.VMEM((NC, ROWS, HEAD), bf16),
            pltpu.VMEM((NC - 1, ROWS, HEAD), bf16),
            pltpu.VMEM((NC - 1, ROWS, HEAD), bf16),
            pltpu.VMEM((2, PACK, HEAD), f32),
            pltpu.VMEM((2, PACK, HEAD), bf16),
            pltpu.VMEM((2, PACK, HEAD), bf16),
            pltpu.VMEM((2, PACK, HEAD), bf16),
            pltpu.VMEM((2, NC - 1, PACK, HEAD), bf16),
            pltpu.VMEM((2, 2, PACK, HEAD), bf16),
            pltpu.VMEM((ROWS, HEAD), f32),
            pltpu.VMEM((ROWS, HEAD), f32),
            pltpu.VMEM((ROWS, HEAD), f32),
            dma((8,)),
            dma((2, NZ - 1)), dma((2, NZ - 1)),
            dma((2, NX - 1)), dma((2, NX - 1)),
            dma((2,)), dma((2,)),
            dma((2, NZ - 1)), dma((2, NZ - 1)),
            dma((NC,)), dma((NC,)),
            dma((NC - 1,)), dma((NC - 1,)),
            dma((2, NC + 1)), dma((2, NC + 1)),
        ],
        compiler_params=pltpu.CompilerParams(
            collective_id=0, has_side_effects=True, vmem_limit_bytes=60 * 1024 * 1024
        ),
        name="key_rows",
    )(
        store_index,
        offsets,
        tenant,
        tokens,
        frozen_key_weight,
        store_a[0],
        store_b[0].T,
        bank_a,
        bank_b.T,
    )


def solution(mesh):
    in_specs = (
        P("rep", "tp"),
        P("rep"),
        P("rep"),
        P(),
        P("tp", None),
        P("rep", None, "tp"),
        P("rep", "tp", None),
        P(None, "tp"),
        P("tp", None),
    )
    return jax.shard_map(
        per_device, mesh=mesh, in_specs=in_specs, out_specs=P("rep", "tp"), check_vma=False
    )
```

```python
import functools
import math

import jax
import jax.numpy as jnp
from jax import lax
from jax.experimental import pallas as pl
from jax.experimental.pallas import tpu as pltpu
from jax.sharding import PartitionSpec as P

MESH = pl.DeviceIdType.MESH
SCALE = 2.0
NY, NZ, NX = 2, 8, 4
NC = 4
ROWS = 384
FEAT = 1536
HEAD = 128
RANK = 64
HALF = ROWS // 2
PACK = ROWS // 4
TILES = (4, 3)
CHUNK = FEAT // 2


def kernel(
    home,
    index_hbm, offset_hbm, tenant_hbm, tok_hbm, w_hbm, a_hbm, bt_hbm, ba_hbm, bbt_hbm, out_ref,
    index_ref, offset_ref, tenant_ref, tok, w, a_raw, bt_raw, bank, ranks, bank_up, up,
    z_src0, z_src1, z_got0, z_got1, x_got0, x_got1, g_got0, g_got1,
    mine, pair_src, pair_got, part_src, part_got,
    l_mine, l_src, l_got, l_chip, l_chips, l_all,
    acc, cos2, sin2,
    load_sem, ready,
    z_ss, z_rs, x_ss, x_rs, y_ss, y_rs, g_ss, g_rs, q_ss, q_rs, p_ss, p_rs, l_ss, l_rs,
):
    bf16, f32 = jnp.bfloat16, jnp.float32
    rep, t = lax.axis_index("rep"), lax.axis_index("tp")
    yh, z, x = rep // (NZ * NX), (rep // NX) % NZ, rep % NX
    yl, core = t // 2, t % 2

    def at(yh_, z_, x_):
        return (yh_ * NZ + z_) * NX + x_

    z_of = [(z + k) % NZ for k in range(1, NZ)]
    x_of = [(x + k) % NX for k in range(1, NX)]
    c_of = [(yl + k) % NC for k in range(1, NC)]
    z_peers = [(at(yh, q, x), t) for q in z_of]
    x_peers = [(at(yh, z, q), t) for q in x_of]
    y_peer = (at(1 - yh, z, x), t)
    c_peers = [(rep, 2 * q + core) for q in c_of]
    twin = (rep, 2 * yl + 1 - core)

    at_home = yh == home
    barrier = pltpu.get_barrier_semaphore()
    peers = z_peers + x_peers + c_peers + [twin]
    for peer in peers:
        pl.semaphore_signal(barrier, inc=1, device_id=peer, device_id_type=MESH)

    @pl.when(yh == 0)
    def _():
        pl.semaphore_signal(barrier, inc=1, device_id=y_peer, device_id_type=MESH)

    bank_up[...] = jnp.zeros_like(bank_up)
    up[...] = jnp.zeros_like(up)
    loads = [
        pltpu.make_async_copy(src, dst, load_sem.at[i])
        for i, (src, dst) in enumerate(
            [
                (a_hbm, a_raw),
                (bt_hbm, bt_raw),
                (tok_hbm, tok),
                (ba_hbm, bank.at[pl.ds(0, RANK)]),
                (ba_hbm, bank.at[pl.ds(RANK, RANK)]),
                (w_hbm, w),
                (bbt_hbm, bank_up.at[pl.ds(0, RANK), pl.ds(0, HEAD)]),
                (bbt_hbm, bank_up.at[pl.ds(RANK, RANK), pl.ds(HEAD, HEAD)]),
                (index_hbm, index_ref),
                (offset_hbm, offset_ref),
                (tenant_hbm, tenant_ref),
            ]
        )
    ]
    for load in loads:
        load.start()

    z_src, z_got, x_got, g_got = (
        (z_src0, z_src1), (z_got0, z_got1), (x_got0, x_got1), (g_got0, g_got1)
    )

    def tile(q, chunk, j):
        return 16 * (q // 2), chunk * CHUNK + ((q % 2) * 3 + j) * HEAD

    loads[0].wait()
    loads[1].wait()
    for chunk in range(2):
        for q in range(NZ):
            for j in range(3):
                row, column = tile(q, chunk, j)
                z_src[chunk][q, 16 * j : 16 * (j + 1), :] = a_raw[
                    row : row + 16, column : column + HEAD
                ].astype(bf16)
            if chunk == 0:
                row = 16 * (q // 2)
                z_src[chunk][q, 48:64, :] = bt_raw[row : row + 16, :].astype(bf16)

    pl.semaphore_wait(barrier, len(peers) + yh)
    if home == 0:

        @pl.when(yh == 1)
        def _():
            pl.semaphore_signal(ready, inc=1, device_id=y_peer, device_id_type=MESH)

    started = []

    def remote(src, dst, ss, rs, peer):
        return pltpu.make_async_remote_copy(
            src_ref=src, dst_ref=dst, send_sem=ss, recv_sem=rs, device_id=peer, device_id_type=MESH
        )

    def send(*args):
        copy = remote(*args)
        copy.start()
        started.append(copy)
        return copy

    def arrived(copies):
        for copy in copies:
            copy.wait_recv()

    z_copies = [
        [
            remote(
                z_src[chunk].at[z_of[i]], z_got[chunk].at[z],
                z_ss.at[chunk, i], z_rs.at[chunk, i], z_peers[i],
            )
            for i in range(NZ - 1)
        ]
        for chunk in range(2)
    ]
    x_copies = [
        [
            remote(
                x_got[chunk].at[x], x_got[chunk].at[x],
                x_ss.at[chunk, i], x_rs.at[chunk, i], x_peers[i],
            )
            for i in range(NX - 1)
        ]
        for chunk in range(2)
    ]
    y_copies = [
        remote(g_got[chunk].at[z], g_got[chunk].at[z], y_ss.at[chunk], y_rs.at[chunk], y_peer)
        for chunk in range(2)
    ]

    @pl.when(at_home)
    def _():
        for chunk in range(2):
            for copy in z_copies[chunk]:
                copy.start()
        for chunk in range(2):
            z_got[chunk][z] = z_src[chunk][z]

    lane = lax.broadcasted_iota(jnp.int32, (PACK, HEAD), 1)
    left = lane < RANK

    def low_start(s, low):
        halves = [
            jnp.where(left, low[HALF * h : HALF * h + PACK], low[HALF * h + PACK : HALF * (h + 1)])
            for h in range(2)
        ]
        l_mine[s] = jnp.where(core == 0, halves[0], halves[1])
        l_src[s] = jnp.where(core == 0, halves[1], halves[0]).astype(bf16)
        return send(l_src.at[s], l_got.at[s], l_ss.at[s, 0], l_rs.at[s, 0], twin)

    def low_spread(s, copy):
        copy.wait_recv()
        l_chip[s] = (l_mine[s] + l_got[s].astype(f32)).astype(bf16)
        return [
            send(l_chip.at[s], l_chips.at[s, i], l_ss.at[s, 1 + i], l_rs.at[s, 1 + i], c_peers[i])
            for i in range(NC - 1)
        ]

    def low_join(s, copies):
        total = l_chip[s].astype(f32)
        for i, copy in enumerate(copies):
            copy.wait_recv()
            total = total + l_chips[s, i].astype(f32)
        l_all[s, core] = total.astype(bf16)
        return send(l_all.at[s, core], l_all.at[s, core], l_ss.at[s, NC], l_rs.at[s, NC], twin)

    def expanded(s, copy, ups):
        copy.wait_recv()
        parts = []
        for h in range(2):
            both = jnp.dot(l_all[s, h], ups[...], preferred_element_type=f32)
            parts += [both[:, :HEAD], both[:, HEAD:]]
        return SCALE * jnp.concatenate(parts, axis=0)

    def times_ranks(a, b):
        return lax.dot_general(a, b, (((1,), (1,)), ((), ())), preferred_element_type=f32)

    loads[2].wait()
    loads[3].wait()
    loads[4].wait()
    bank_step = low_start(0, times_ranks(tok[...], bank[...]))

    loads[5].wait()
    order = c_of + [yl]
    pair_copies = []
    part_copies = []

    def passed(k):
        pair_copies[k].wait_recv()
        total = mine[k] + pair_got[k].astype(f32)
        if k == NC - 1:
            acc[...] = total
            return
        part_src[k] = total.astype(bf16)
        part_copies.append(
            send(part_src.at[k], part_got.at[k], p_ss.at[k], p_rs.at[k], c_peers[k])
        )

    for k, q in enumerate(order):
        column = pl.multiple_of(q * 2 * HEAD, 2 * HEAD)
        both = jnp.dot(tok[...], w[:, pl.ds(column, 2 * HEAD)], preferred_element_type=f32)
        mine[k] = jnp.where(core == 0, both[:, :HEAD], both[:, HEAD:])
        pair_src[k] = jnp.where(core == 0, both[:, HEAD:], both[:, :HEAD]).astype(bf16)
        pair_copies.append(send(pair_src.at[k], pair_got.at[k], q_ss.at[k], q_rs.at[k], twin))
        if k == 1:
            bank_step = low_spread(0, bank_step)
        if k >= 1:
            passed(k - 1)
    passed(NC - 1)

    loads[9].wait()
    wide = lax.broadcasted_iota(jnp.int32, (HALF, HEAD), 1)
    row = lax.broadcasted_iota(jnp.int32, (HALF, HEAD), 0)
    row = jnp.where(wide < HEAD // 2, row, row + HALF)
    freq = jnp.exp((wide % (HEAD // 2)).astype(f32) * (-2.0 * math.log(1000000.0) / HEAD))
    angle = (offset_ref[0] + row).astype(f32) * freq
    first = wide < HEAD // 2
    cosine, sine = jnp.cos(angle), jnp.sin(angle)
    turned_cos, turned_sin = pltpu.roll(cosine, HEAD // 2, 1), pltpu.roll(sine, HEAD // 2, 1)
    cos2[0:HALF, :] = jnp.where(first, cosine, turned_cos)
    cos2[HALF:, :] = jnp.where(first, turned_cos, cosine)
    sin2[0:HALF, :] = jnp.where(first, -sine, turned_sin)
    sin2[HALF:, :] = jnp.where(first, -turned_sin, sine)

    loads[8].wait()

    @pl.when(at_home)
    def _():
        root = index_ref[0]
        root_z, root_x = (root // NX) % NZ, root % NX
        for chunk in range(2):
            arrived(z_copies[chunk])
            x_got[chunk][x] = z_got[chunk][root_z]
            for copy in x_copies[chunk]:
                copy.start()
        for chunk in range(2):
            arrived(x_copies[chunk])
            g_got[chunk][z] = x_got[chunk][root_x]
            if chunk == 0 and home == 0:
                pl.semaphore_wait(ready, 1)
            y_copies[chunk].start()

    bank_step = low_join(0, bank_step)

    loads[10].wait()
    eye = lax.broadcasted_iota(jnp.int32, (HEAD, HEAD), 0) == lax.broadcasted_iota(
        jnp.int32, (HEAD, HEAD), 1
    )
    tenant = jnp.concatenate(
        [
            jnp.sum(
                jnp.where(eye, tenant_ref[pl.ds(HEAD * i, HEAD)].reshape(1, HEAD), 0).astype(f32),
                axis=1,
                keepdims=True,
            )
            for i in range(ROWS // HEAD)
        ],
        axis=0,
    )

    g_copies = []
    for chunk in range(2):

        @pl.when(jnp.logical_not(at_home))
        def _(chunk=chunk):
            y_copies[chunk].wait_recv()

        g_copies.append(
            [
                send(
                    g_got[chunk].at[z], g_got[chunk].at[z],
                    g_ss.at[chunk, i], g_rs.at[chunk, i], z_peers[i],
                )
                for i in range(NZ - 1)
            ]
        )

    total = acc[...]
    for k, copy in enumerate(part_copies):
        copy.wait_recv()
        total = total + part_got[k].astype(f32)
    loads[6].wait()
    loads[7].wait()
    acc[...] = total + jnp.where(tenant == 1.0, expanded(0, bank_step, bank_up), 0.0)

    low = None
    for chunk in range(2):
        arrived(g_copies[chunk])
        for q in range(NZ):
            for j in range(3):
                row, column = tile(q, chunk, j)
                value = g_got[chunk][q, 16 * j : 16 * (j + 1), :]
                ranks[row : row + 16, column : column + HEAD] = value
                ranks[RANK + row : RANK + row + 16, column : column + HEAD] = value
        columns = slice(chunk * CHUNK, (chunk + 1) * CHUNK)
        term = times_ranks(tok[:, columns], ranks[:, columns])
        low = term if low is None else low + term
    store_step = low_start(1, low)
    for q in range(0, NZ, 2):
        row = 16 * (q // 2)
        value = g_got[0][q, 48:64, :]
        up[row : row + 16, 0:HEAD] = value
        up[RANK + row : RANK + row + 16, HEAD:] = value
    store_step = low_spread(1, store_step)
    store_step = low_join(1, store_step)
    adapted = acc[...] + jnp.where(tenant == 2.0, expanded(1, store_step, up), 0.0)
    swapped = pltpu.roll(adapted, HEAD // 2, 1)
    out_ref[...] = (adapted * cos2[...] + swapped * sin2[...]).astype(bf16)
    for copy in started:
        copy.wait_send()

    @pl.when(at_home)
    def _():
        for copy in z_copies[0] + z_copies[1] + x_copies[0] + x_copies[1] + y_copies:
            copy.wait_send()


def key_rows(home, *args):
    bf16, f32 = jnp.bfloat16, jnp.float32
    vmem = pl.BlockSpec(memory_space=pltpu.VMEM)
    hbm = pl.BlockSpec(memory_space=pl.ANY)
    dma = pltpu.SemaphoreType.DMA

    def slices(n):
        return [pltpu.VMEM((n, 16 * tiles, HEAD), bf16) for tiles in TILES]

    return pl.pallas_call(
        functools.partial(kernel, home),
        out_shape=jax.ShapeDtypeStruct((ROWS, HEAD), bf16),
        in_specs=[hbm] * 9,
        out_specs=vmem,
        scratch_shapes=[
            pltpu.SMEM((1,), jnp.int32),
            pltpu.SMEM((1,), jnp.int32),
            pltpu.VMEM((ROWS,), jnp.int32),
            pltpu.VMEM((ROWS, FEAT), bf16),
            pltpu.VMEM((FEAT, 2 * NC * HEAD), bf16),
            pltpu.VMEM((RANK, FEAT), f32),
            pltpu.VMEM((RANK, HEAD), f32),
            pltpu.VMEM((2 * RANK, FEAT), bf16),
            pltpu.VMEM((2 * RANK, FEAT), bf16),
            pltpu.VMEM((2 * RANK, 2 * HEAD), bf16),
            pltpu.VMEM((2 * RANK, 2 * HEAD), bf16),
            *slices(NZ), *slices(NZ), *slices(NX), *slices(NZ),
            pltpu.VMEM((NC, ROWS, HEAD), f32),
            pltpu.VMEM((NC, ROWS, HEAD), bf16),
            pltpu.VMEM((NC, ROWS, HEAD), bf16),
            pltpu.VMEM((NC - 1, ROWS, HEAD), bf16),
            pltpu.VMEM((NC - 1, ROWS, HEAD), bf16),
            pltpu.VMEM((2, PACK, HEAD), f32),
            pltpu.VMEM((2, PACK, HEAD), bf16),
            pltpu.VMEM((2, PACK, HEAD), bf16),
            pltpu.VMEM((2, PACK, HEAD), bf16),
            pltpu.VMEM((2, NC - 1, PACK, HEAD), bf16),
            pltpu.VMEM((2, 2, PACK, HEAD), bf16),
            pltpu.VMEM((ROWS, HEAD), f32),
            pltpu.VMEM((ROWS, HEAD), f32),
            pltpu.VMEM((ROWS, HEAD), f32),
            dma((11,)),
            pltpu.SemaphoreType.REGULAR,
            dma((2, NZ - 1)), dma((2, NZ - 1)),
            dma((2, NX - 1)), dma((2, NX - 1)),
            dma((2,)), dma((2,)),
            dma((2, NZ - 1)), dma((2, NZ - 1)),
            dma((NC,)), dma((NC,)),
            dma((NC - 1,)), dma((NC - 1,)),
            dma((2, NC + 1)), dma((2, NC + 1)),
        ],
        compiler_params=pltpu.CompilerParams(
            collective_id=home, has_side_effects=True, vmem_limit_bytes=60 * 1024 * 1024
        ),
        name=f"key_rows_{home}",
    )(*args)


def per_device(
    tokens, tenant, offsets, store_index, frozen_key_weight, store_a, store_b, bank_a, bank_b
):
    return lax.cond(
        store_index[0] < NZ * NX,
        functools.partial(key_rows, 0),
        functools.partial(key_rows, 1),
        store_index,
        offsets,
        tenant,
        tokens,
        frozen_key_weight,
        store_a[0],
        store_b[0].T,
        bank_a,
        bank_b.T,
    )


def solution(mesh):
    in_specs = (
        P("rep", "tp"),
        P("rep"),
        P("rep"),
        P(),
        P("tp", None),
        P("rep", None, "tp"),
        P("rep", "tp", None),
        P(None, "tp"),
        P("tp", None),
    )
    return jax.shard_map(
        per_device, mesh=mesh, in_specs=in_specs, out_specs=P("rep", "tp"), check_vma=False
    )
```

```python
import functools
import math

import jax
import jax.numpy as jnp
from jax import lax
from jax.experimental import pallas as pl
from jax.experimental.pallas import tpu as pltpu
from jax.sharding import PartitionSpec as P

MESH = pl.DeviceIdType.MESH
SCALE = 2.0
NY, NZ, NX = 2, 8, 4
NC = 4
ROWS = 384
FEAT = 1536
HEAD = 128
RANK = 64
HALF = ROWS // 2
PACK = ROWS // 4
NH = 4
NL = NZ - NH
WIDE = 6
TILES = (WIDE + 1, WIDE)
CHUNK = FEAT // 2


def kernel(
    root_z,
    index_hbm, offset_hbm, tenant_hbm, tok_hbm, w_hbm, a_hbm, bt_hbm, ba_hbm, bbt_hbm, out_ref,
    index_ref, offset_ref, tenant_ref, tok, w, a_raw, bt_raw, bank, ranks, bank_up, up,
    src0, src1, x_got0, x_got1, y_got0, y_got1, g_got0, g_got1,
    mine, pair_src, pair_got, part_src, part_got,
    l_mine, l_src, l_got, l_chip, l_chips, l_all,
    acc, cos2, sin2,
    load_sem, ready,
    h_ss, h_rs, x_ss, x_rs, y_ss, y_rs, g_ss, g_rs, q_ss, q_rs, p_ss, p_rs, l_ss, l_rs,
):
    bf16, f32 = jnp.bfloat16, jnp.float32
    rep, t = lax.axis_index("rep"), lax.axis_index("tp")
    yh, z, x = rep // (NZ * NX), (rep // NX) % NZ, rep % NX
    yl, core = t // 2, t % 2

    def at(yh_, z_, x_):
        return (yh_ * NZ + z_) * NX + x_

    x_of = [(x + k) % NX for k in range(1, NX)]
    c_of = [(yl + k) % NC for k in range(1, NC)]
    holder, source = z < NH, z == root_z
    h_of = [(z + k) % NH for k in range(1, NH)]
    h_peers = [(at(yh, q, x), t) for q in h_of]
    holders = [(at(yh, q, x), t) for q in range(NH)]
    late_peers = [(at(yh, NH + q, x), t) for q in range(NL)]
    x_peers = [(at(yh, z, q), t) for q in x_of]
    y_peer = (at(1 - yh, z, x), t)
    c_peers = [(rep, 2 * q + core) for q in c_of]
    twin = (rep, 2 * yl + 1 - core)

    barrier = pltpu.get_barrier_semaphore()

    def greet(peers):
        for peer in peers:
            pl.semaphore_signal(barrier, inc=1, device_id=peer, device_id_type=MESH)

    greet(c_peers + [twin])

    @pl.when(holder)
    def _():
        greet(h_peers + x_peers + [y_peer] + late_peers)

    bank_up[...] = jnp.zeros_like(bank_up)
    up[...] = jnp.zeros_like(up)
    loads = [
        pltpu.make_async_copy(src, dst, load_sem.at[i])
        for i, (src, dst) in enumerate(
            [
                (tok_hbm, tok),
                (ba_hbm, bank.at[pl.ds(0, RANK)]),
                (ba_hbm, bank.at[pl.ds(RANK, RANK)]),
                (w_hbm, w),
                (bbt_hbm, bank_up.at[pl.ds(0, RANK), pl.ds(0, HEAD)]),
                (bbt_hbm, bank_up.at[pl.ds(RANK, RANK), pl.ds(HEAD, HEAD)]),
                (index_hbm, index_ref),
                (offset_hbm, offset_ref),
                (tenant_hbm, tenant_ref),
                (a_hbm, a_raw),
                (bt_hbm, bt_raw),
            ]
        )
    ]

    @pl.when(source)
    def _():
        for load in loads[9:]:
            load.start()

    for load in loads[:9]:
        load.start()

    src, x_got, y_got, g_got = (
        (src0, src1), (x_got0, x_got1), (y_got0, y_got1), (g_got0, g_got1)
    )

    @pl.when(source)
    def _():
        for load in loads[9:]:
            load.wait()
        for chunk in range(2):
            for h in range(NH):
                for j in range(WIDE):
                    column = chunk * CHUNK + j * HEAD
                    src[chunk][h, 16 * j : 16 * (j + 1), :] = a_raw[
                        16 * h : 16 * (h + 1), column : column + HEAD
                    ].astype(bf16)
                if chunk == 0:
                    src[chunk][h, 16 * WIDE :, :] = bt_raw[16 * h : 16 * (h + 1), :].astype(bf16)
            if root_z < NH:
                x_got[chunk][x] = src[chunk][root_z]

    replica = NC
    pl.semaphore_wait(barrier, replica + jnp.where(holder, NH + NX - 1, NH))

    @pl.when(jnp.logical_not(holder))
    def _():
        for peer in holders:
            pl.semaphore_signal(ready.at[z - NH], inc=1, device_id=peer, device_id_type=MESH)

    started = []

    def remote(src, dst, ss, rs, peer):
        return pltpu.make_async_remote_copy(
            src_ref=src, dst_ref=dst, send_sem=ss, recv_sem=rs, device_id=peer, device_id_type=MESH
        )

    def send(*args):
        copy = remote(*args)
        copy.start()
        started.append(copy)
        return copy

    def arrived(copies):
        for copy in copies:
            copy.wait_recv()

    far = [h for h in range(NH) if h != root_z]
    h_copies = [
        [
            remote(
                src[chunk].at[h], x_got[chunk].at[x], h_ss.at[chunk, h], h_rs.at[chunk], holders[h]
            )
            for h in far
        ]
        for chunk in range(2)
    ]
    x_copies = [
        [
            remote(
                x_got[chunk].at[x], x_got[chunk].at[x],
                x_ss.at[chunk, i], x_rs.at[chunk, i], x_peers[i],
            )
            for i in range(NX - 1)
        ]
        for chunk in range(2)
    ]
    y_copies = [
        remote(y_got[chunk].at[yh], y_got[chunk].at[yh], y_ss.at[chunk], y_rs.at[chunk], y_peer)
        for chunk in range(2)
    ]

    def g_copies(chunk, first, peers):
        return [
            remote(
                g_got[chunk].at[z], g_got[chunk].at[z],
                g_ss.at[chunk, first + i], g_rs.at[chunk, z], peer,
            )
            for i, peer in enumerate(peers)
        ]

    @pl.when(source)
    def _():
        for chunk in range(2):
            for copy in h_copies[chunk]:
                copy.start()

    lane = lax.broadcasted_iota(jnp.int32, (PACK, HEAD), 1)
    left = lane < RANK

    def low_start(s, low):
        halves = [
            jnp.where(left, low[HALF * h : HALF * h + PACK], low[HALF * h + PACK : HALF * (h + 1)])
            for h in range(2)
        ]
        l_mine[s] = jnp.where(core == 0, halves[0], halves[1])
        l_src[s] = jnp.where(core == 0, halves[1], halves[0]).astype(bf16)
        return send(l_src.at[s], l_got.at[s], l_ss.at[s, 0], l_rs.at[s, 0], twin)

    def low_spread(s, copy):
        copy.wait_recv()
        l_chip[s] = (l_mine[s] + l_got[s].astype(f32)).astype(bf16)
        return [
            send(l_chip.at[s], l_chips.at[s, i], l_ss.at[s, 1 + i], l_rs.at[s, 1 + i], c_peers[i])
            for i in range(NC - 1)
        ]

    def low_join(s, copies):
        total = l_chip[s].astype(f32)
        for i, copy in enumerate(copies):
            copy.wait_recv()
            total = total + l_chips[s, i].astype(f32)
        l_all[s, core] = total.astype(bf16)
        return send(l_all.at[s, core], l_all.at[s, core], l_ss.at[s, NC], l_rs.at[s, NC], twin)

    def expanded(s, copy, ups):
        copy.wait_recv()
        parts = []
        for h in range(2):
            both = jnp.dot(l_all[s, h], ups[...], preferred_element_type=f32)
            parts += [both[:, :HEAD], both[:, HEAD:]]
        return SCALE * jnp.concatenate(parts, axis=0)

    def times_ranks(a, b):
        return lax.dot_general(a, b, (((1,), (1,)), ((), ())), preferred_element_type=f32)

    loads[0].wait()
    loads[1].wait()
    loads[2].wait()
    bank_step = low_start(0, times_ranks(tok[...], bank[...]))

    loads[3].wait()
    order = c_of + [yl]
    pair_copies = []
    part_copies = []

    def passed(k):
        pair_copies[k].wait_recv()
        total = mine[k] + pair_got[k].astype(f32)
        if k == NC - 1:
            acc[...] = total
            return
        part_src[k] = total.astype(bf16)
        part_copies.append(
            send(part_src.at[k], part_got.at[k], p_ss.at[k], p_rs.at[k], c_peers[k])
        )

    for k, q in enumerate(order):
        column = pl.multiple_of(q * 2 * HEAD, 2 * HEAD)
        both = jnp.dot(tok[...], w[:, pl.ds(column, 2 * HEAD)], preferred_element_type=f32)
        mine[k] = jnp.where(core == 0, both[:, :HEAD], both[:, HEAD:])
        pair_src[k] = jnp.where(core == 0, both[:, HEAD:], both[:, :HEAD]).astype(bf16)
        pair_copies.append(send(pair_src.at[k], pair_got.at[k], q_ss.at[k], q_rs.at[k], twin))
        if k == 1:
            bank_step = low_spread(0, bank_step)
        if k >= 1:
            passed(k - 1)
    passed(NC - 1)

    loads[7].wait()
    wide = lax.broadcasted_iota(jnp.int32, (HALF, HEAD), 1)
    row = lax.broadcasted_iota(jnp.int32, (HALF, HEAD), 0)
    row = jnp.where(wide < HEAD // 2, row, row + HALF)
    freq = jnp.exp((wide % (HEAD // 2)).astype(f32) * (-2.0 * math.log(1000000.0) / HEAD))
    angle = (offset_ref[0] + row).astype(f32) * freq
    first = wide < HEAD // 2
    cosine, sine = jnp.cos(angle), jnp.sin(angle)
    turned_cos, turned_sin = pltpu.roll(cosine, HEAD // 2, 1), pltpu.roll(sine, HEAD // 2, 1)
    cos2[0:HALF, :] = jnp.where(first, cosine, turned_cos)
    cos2[HALF:, :] = jnp.where(first, turned_cos, cosine)
    sin2[0:HALF, :] = jnp.where(first, -sine, turned_sin)
    sin2[HALF:, :] = jnp.where(first, -turned_sin, sine)

    loads[6].wait()

    @pl.when(holder)
    def _():
        root_x = index_ref[0] % NX
        for chunk in range(2):

            @pl.when(jnp.logical_not(source))
            def _(chunk=chunk):
                h_copies[chunk][0].wait_recv()

            for copy in x_copies[chunk]:
                copy.start()
        for chunk in range(2):
            arrived(x_copies[chunk])
            y_got[chunk][yh] = x_got[chunk][root_x]
            y_copies[chunk].start()

    bank_step = low_join(0, bank_step)

    loads[8].wait()
    eye = lax.broadcasted_iota(jnp.int32, (HEAD, HEAD), 0) == lax.broadcasted_iota(
        jnp.int32, (HEAD, HEAD), 1
    )
    tenant = jnp.concatenate(
        [
            jnp.sum(
                jnp.where(eye, tenant_ref[pl.ds(HEAD * i, HEAD)].reshape(1, HEAD), 0).astype(f32),
                axis=1,
                keepdims=True,
            )
            for i in range(ROWS // HEAD)
        ],
        axis=0,
    )

    @pl.when(holder)
    def _():
        root_y = index_ref[0] // (NZ * NX)
        for chunk in range(2):
            y_copies[chunk].wait_recv()
            g_got[chunk][z] = y_got[chunk][root_y]
            for copy in g_copies(chunk, 0, h_peers):
                copy.start()
        for i in range(NL):
            pl.semaphore_wait(ready.at[i], 1)
        for chunk in range(2):
            for copy in g_copies(chunk, NH - 1, late_peers):
                copy.start()

    total = acc[...]
    for k, copy in enumerate(part_copies):
        copy.wait_recv()
        total = total + part_got[k].astype(f32)
    loads[4].wait()
    loads[5].wait()
    acc[...] = total + jnp.where(tenant == 1.0, expanded(0, bank_step, bank_up), 0.0)

    low = None
    for chunk in range(2):
        for h in range(NH):

            @pl.when(z != h)
            def _(chunk=chunk, h=h):
                remote(
                    g_got[chunk].at[h], g_got[chunk].at[h],
                    g_ss.at[chunk, 0], g_rs.at[chunk, h], y_peer,
                ).wait_recv()

            for j in range(WIDE):
                column = chunk * CHUNK + j * HEAD
                value = g_got[chunk][h, 16 * j : 16 * (j + 1), :]
                for row in (16 * h, RANK + 16 * h):
                    ranks[row : row + 16, column : column + HEAD] = value
        columns = slice(chunk * CHUNK, (chunk + 1) * CHUNK)
        term = times_ranks(tok[:, columns], ranks[:, columns])
        low = term if low is None else low + term
    store_step = low_start(1, low)
    for h in range(NH):
        row = 16 * h
        value = g_got[0][h, 16 * WIDE :, :]
        up[row : row + 16, 0:HEAD] = value
        up[RANK + row : RANK + row + 16, HEAD:] = value
    store_step = low_spread(1, store_step)
    store_step = low_join(1, store_step)
    adapted = acc[...] + jnp.where(tenant == 2.0, expanded(1, store_step, up), 0.0)
    swapped = pltpu.roll(adapted, HEAD // 2, 1)
    out_ref[...] = (adapted * cos2[...] + swapped * sin2[...]).astype(bf16)
    for copy in started:
        copy.wait_send()

    @pl.when(source)
    def _():
        for copy in h_copies[0] + h_copies[1]:
            copy.wait_send()

    @pl.when(holder)
    def _():
        for chunk in range(2):
            for copy in x_copies[chunk] + [y_copies[chunk]] + g_copies(chunk, 0, h_peers + late_peers):
                copy.wait_send()


def key_rows(root_z, *args):
    bf16, f32 = jnp.bfloat16, jnp.float32
    vmem = pl.BlockSpec(memory_space=pltpu.VMEM)
    hbm = pl.BlockSpec(memory_space=pl.ANY)
    dma = pltpu.SemaphoreType.DMA

    def slices(n):
        return [pltpu.VMEM((n, 16 * tiles, HEAD), bf16) for tiles in TILES]

    return pl.pallas_call(
        functools.partial(kernel, root_z),
        out_shape=jax.ShapeDtypeStruct((ROWS, HEAD), bf16),
        in_specs=[hbm] * 9,
        out_specs=vmem,
        scratch_shapes=[
            pltpu.SMEM((1,), jnp.int32),
            pltpu.SMEM((1,), jnp.int32),
            pltpu.VMEM((ROWS,), jnp.int32),
            pltpu.VMEM((ROWS, FEAT), bf16),
            pltpu.VMEM((FEAT, 2 * NC * HEAD), bf16),
            pltpu.VMEM((RANK, FEAT), f32),
            pltpu.VMEM((RANK, HEAD), f32),
            pltpu.VMEM((2 * RANK, FEAT), bf16),
            pltpu.VMEM((2 * RANK, FEAT), bf16),
            pltpu.VMEM((2 * RANK, 2 * HEAD), bf16),
            pltpu.VMEM((2 * RANK, 2 * HEAD), bf16),
            *slices(NH), *slices(NX), *slices(NY), *slices(NH),
            pltpu.VMEM((NC, ROWS, HEAD), f32),
            pltpu.VMEM((NC, ROWS, HEAD), bf16),
            pltpu.VMEM((NC, ROWS, HEAD), bf16),
            pltpu.VMEM((NC - 1, ROWS, HEAD), bf16),
            pltpu.VMEM((NC - 1, ROWS, HEAD), bf16),
            pltpu.VMEM((2, PACK, HEAD), f32),
            pltpu.VMEM((2, PACK, HEAD), bf16),
            pltpu.VMEM((2, PACK, HEAD), bf16),
            pltpu.VMEM((2, PACK, HEAD), bf16),
            pltpu.VMEM((2, NC - 1, PACK, HEAD), bf16),
            pltpu.VMEM((2, 2, PACK, HEAD), bf16),
            pltpu.VMEM((ROWS, HEAD), f32),
            pltpu.VMEM((ROWS, HEAD), f32),
            pltpu.VMEM((ROWS, HEAD), f32),
            dma((11,)),
            pltpu.SemaphoreType.REGULAR((NL,)),
            dma((2, NH)), dma((2,)),
            dma((2, NX - 1)), dma((2, NX - 1)),
            dma((2,)), dma((2,)),
            dma((2, NZ - 1)), dma((2, NH)),
            dma((NC,)), dma((NC,)),
            dma((NC - 1,)), dma((NC - 1,)),
            dma((2, NC + 1)), dma((2, NC + 1)),
        ],
        compiler_params=pltpu.CompilerParams(
            collective_id=root_z, has_side_effects=True, vmem_limit_bytes=60 * 1024 * 1024
        ),
        name=f"key_rows_{root_z}",
    )(*args)


def per_device(
    tokens, tenant, offsets, store_index, frozen_key_weight, store_a, store_b, bank_a, bank_b
):
    return lax.switch(
        lax.rem(lax.div(store_index[0], NX), NZ),
        [functools.partial(key_rows, z) for z in range(NZ)],
        store_index,
        offsets,
        tenant,
        tokens,
        frozen_key_weight,
        store_a[0],
        store_b[0].T,
        bank_a,
        bank_b.T,
    )


def solution(mesh):
    in_specs = (
        P("rep", "tp"),
        P("rep"),
        P("rep"),
        P(),
        P("tp", None),
        P("rep", None, "tp"),
        P("rep", "tp", None),
        P(None, "tp"),
        P("tp", None),
    )
    return jax.shard_map(
        per_device, mesh=mesh, in_specs=in_specs, out_specs=P("rep", "tp"), check_vma=False
    )
```

```python
import functools
import math

import jax
import jax.numpy as jnp
from jax import lax
from jax.experimental import pallas as pl
from jax.experimental.pallas import tpu as pltpu
from jax.sharding import PartitionSpec as P

MESH = pl.DeviceIdType.MESH
SCALE = 2.0
NY, NZ, NX = 2, 8, 4
NC = 4
ROWS = 384
FEAT = 1536
HEAD = 128
RANK = 64
HALF = ROWS // 2
PACK = ROWS // 4
NH = 4
NL = NZ - NH
EARLY = 0
WIDE = 6
TILES = (WIDE + 1, WIDE)
CHUNK = FEAT // 2


def kernel(
    root_z,
    index_hbm, offset_hbm, tenant_hbm, tok_hbm, w_hbm, a_hbm, bt_hbm, ba_hbm, bbt_hbm, out_ref,
    index_ref, offset_ref, tenant_ref, tok, w, a_raw, bt_raw, bank, ranks, bank_up, up,
    src0, src1, x_got0, x_got1, y_got0, y_got1, g_got0, g_got1,
    mine, pair_src, pair_got, part_src, part_got,
    l_mine, l_src, l_got, l_chip, l_chips, l_all,
    acc, cos2, sin2,
    load_sem, ready,
    h_ss, h_rs, x_ss, x_rs, y_ss, y_rs, g_ss, g_rs, q_ss, q_rs, p_ss, p_rs, l_ss, l_rs,
):
    bf16, f32 = jnp.bfloat16, jnp.float32
    rep, t = lax.axis_index("rep"), lax.axis_index("tp")
    yh, z, x = rep // (NZ * NX), (rep // NX) % NZ, rep % NX
    yl, core = t // 2, t % 2

    def at(yh_, z_, x_):
        return (yh_ * NZ + z_) * NX + x_

    x_of = [(x + k) % NX for k in range(1, NX)]
    c_of = [(yl + k) % NC for k in range(1, NC)]
    holder, source = z < NH, z == root_z
    h_of = [(z + k) % NH for k in range(1, NH)]
    h_peers = [(at(yh, q, x), t) for q in h_of]
    holders = [(at(yh, q, x), t) for q in range(NH)]
    late_peers = [(at(yh, NH + q, x), t) for q in range(NL)]
    x_peers = [(at(yh, z, q), t) for q in x_of]
    y_peer = (at(1 - yh, z, x), t)
    c_peers = [(rep, 2 * q + core) for q in c_of]
    twin = (rep, 2 * yl + 1 - core)

    barrier = pltpu.get_barrier_semaphore()

    def greet(peers):
        for peer in peers:
            pl.semaphore_signal(barrier, inc=1, device_id=peer, device_id_type=MESH)

    greet(c_peers + [twin])

    @pl.when(holder)
    def _():
        greet(h_peers + x_peers + [y_peer] + late_peers)

    bank_up[...] = jnp.zeros_like(bank_up)
    up[...] = jnp.zeros_like(up)
    loads = [
        pltpu.make_async_copy(src, dst, load_sem.at[i])
        for i, (src, dst) in enumerate(
            [
                (tok_hbm, tok),
                (ba_hbm, bank.at[pl.ds(0, RANK)]),
                (ba_hbm, bank.at[pl.ds(RANK, RANK)]),
                (w_hbm, w),
                (bbt_hbm, bank_up.at[pl.ds(0, RANK), pl.ds(0, HEAD)]),
                (bbt_hbm, bank_up.at[pl.ds(RANK, RANK), pl.ds(HEAD, HEAD)]),
                (index_hbm, index_ref),
                (offset_hbm, offset_ref),
                (tenant_hbm, tenant_ref),
                (a_hbm, a_raw),
                (bt_hbm, bt_raw),
            ]
        )
    ]

    @pl.when(source)
    def _():
        for load in loads[9:]:
            load.start()

    for load in loads[:9]:
        load.start()

    src, x_got, y_got, g_got = (
        (src0, src1), (x_got0, x_got1), (y_got0, y_got1), (g_got0, g_got1)
    )

    started = []

    def remote(src, dst, ss, rs, peer):
        return pltpu.make_async_remote_copy(
            src_ref=src, dst_ref=dst, send_sem=ss, recv_sem=rs, device_id=peer, device_id_type=MESH
        )

    def send(*args):
        copy = remote(*args)
        copy.start()
        started.append(copy)
        return copy

    def arrived(copies):
        for copy in copies:
            copy.wait_recv()

    far = [h for h in range(NH) if h != root_z]
    h_copies = [
        [
            remote(
                src[chunk].at[h], x_got[chunk].at[x], h_ss.at[chunk, h], h_rs.at[chunk], holders[h]
            )
            for h in far
        ]
        for chunk in range(2)
    ]
    x_copies = [
        [
            remote(
                x_got[chunk].at[x], x_got[chunk].at[x],
                x_ss.at[chunk, i], x_rs.at[chunk, i], x_peers[i],
            )
            for i in range(NX - 1)
        ]
        for chunk in range(2)
    ]
    y_copies = [
        remote(y_got[chunk].at[yh], y_got[chunk].at[yh], y_ss.at[chunk], y_rs.at[chunk], y_peer)
        for chunk in range(2)
    ]

    def g_copies(chunk, first, peers):
        return [
            remote(
                g_got[chunk].at[z], g_got[chunk].at[z],
                g_ss.at[chunk, first + i], g_rs.at[chunk, z], peer,
            )
            for i, peer in enumerate(peers)
        ]

    lane = lax.broadcasted_iota(jnp.int32, (PACK, HEAD), 1)
    left = lane < RANK

    def low_start(s, low):
        halves = [
            jnp.where(left, low[HALF * h : HALF * h + PACK], low[HALF * h + PACK : HALF * (h + 1)])
            for h in range(2)
        ]
        l_mine[s] = jnp.where(core == 0, halves[0], halves[1])
        l_src[s] = jnp.where(core == 0, halves[1], halves[0]).astype(bf16)

    def low_swap(s):
        return send(l_src.at[s], l_got.at[s], l_ss.at[s, 0], l_rs.at[s, 0], twin)

    def low_spread(s, copy):
        copy.wait_recv()
        l_chip[s] = (l_mine[s] + l_got[s].astype(f32)).astype(bf16)
        return [
            send(l_chip.at[s], l_chips.at[s, i], l_ss.at[s, 1 + i], l_rs.at[s, 1 + i], c_peers[i])
            for i in range(NC - 1)
        ]

    def low_join(s, copies):
        total = l_chip[s].astype(f32)
        for i, copy in enumerate(copies):
            copy.wait_recv()
            total = total + l_chips[s, i].astype(f32)
        l_all[s, core] = total.astype(bf16)
        return send(l_all.at[s, core], l_all.at[s, core], l_ss.at[s, NC], l_rs.at[s, NC], twin)

    def expanded(s, copy, ups):
        copy.wait_recv()
        parts = []
        for h in range(2):
            both = jnp.dot(l_all[s, h], ups[...], preferred_element_type=f32)
            parts += [both[:, :HEAD], both[:, HEAD:]]
        return SCALE * jnp.concatenate(parts, axis=0)

    def times_ranks(a, b):
        return lax.dot_general(a, b, (((1,), (1,)), ((), ())), preferred_element_type=f32)

    def greeted():
        replica = NC
        pl.semaphore_wait(barrier, replica + jnp.where(holder, NH + NX - 1, NH))

    def cut():
        for load in loads[9:]:
            load.wait()
        for chunk in range(2):
            for h in range(NH):
                for j in range(WIDE):
                    column = chunk * CHUNK + j * HEAD
                    src[chunk][h, 16 * j : 16 * (j + 1), :] = a_raw[
                        16 * h : 16 * (h + 1), column : column + HEAD
                    ].astype(bf16)
                if chunk == 0:
                    src[chunk][h, 16 * WIDE :, :] = bt_raw[16 * h : 16 * (h + 1), :].astype(bf16)
            if root_z < NH:
                x_got[chunk][x] = src[chunk][root_z]

    def push():
        for chunk in range(2):
            for copy in h_copies[chunk]:
                copy.start()

    source_first = root_z >= NH - 1
    if source_first:

        @pl.when(source)
        def _():
            cut()
            greeted()
            push()

    loads[0].wait()
    loads[1].wait()
    loads[2].wait()
    low_start(0, times_ranks(tok[...], bank[...]))
    loads[3].wait()
    order = c_of + [yl]
    for k, q in enumerate(order):
        column = pl.multiple_of(q * 2 * HEAD, 2 * HEAD)
        both = jnp.dot(tok[...], w[:, pl.ds(column, 2 * HEAD)], preferred_element_type=f32)
        mine[k] = jnp.where(core == 0, both[:, :HEAD], both[:, HEAD:])
        pair_src[k] = jnp.where(core == 0, both[:, HEAD:], both[:, :HEAD]).astype(bf16)

    loads[7].wait()
    wide = lax.broadcasted_iota(jnp.int32, (HALF, HEAD), 1)
    row = lax.broadcasted_iota(jnp.int32, (HALF, HEAD), 0)
    row = jnp.where(wide < HEAD // 2, row, row + HALF)
    freq = jnp.exp((wide % (HEAD // 2)).astype(f32) * (-2.0 * math.log(1000000.0) / HEAD))
    angle = (offset_ref[0] + row).astype(f32) * freq
    first = wide < HEAD // 2
    cosine, sine = jnp.cos(angle), jnp.sin(angle)
    turned_cos, turned_sin = pltpu.roll(cosine, HEAD // 2, 1), pltpu.roll(sine, HEAD // 2, 1)
    cos2[0:HALF, :] = jnp.where(first, cosine, turned_cos)
    cos2[HALF:, :] = jnp.where(first, turned_cos, cosine)
    sin2[0:HALF, :] = jnp.where(first, -sine, turned_sin)
    sin2[HALF:, :] = jnp.where(first, -turned_sin, sine)

    loads[8].wait()
    eye = lax.broadcasted_iota(jnp.int32, (HEAD, HEAD), 0) == lax.broadcasted_iota(
        jnp.int32, (HEAD, HEAD), 1
    )
    tenant = jnp.concatenate(
        [
            jnp.sum(
                jnp.where(eye, tenant_ref[pl.ds(HEAD * i, HEAD)].reshape(1, HEAD), 0).astype(f32),
                axis=1,
                keepdims=True,
            )
            for i in range(ROWS // HEAD)
        ],
        axis=0,
    )

    if source_first:

        @pl.when(jnp.logical_not(source))
        def _():
            greeted()
    else:

        @pl.when(source)
        def _():
            cut()

        greeted()

        @pl.when(source)
        def _():
            push()

    @pl.when(jnp.logical_not(holder))
    def _():
        for peer in holders:
            pl.semaphore_signal(ready.at[z - NH], inc=1, device_id=peer, device_id_type=MESH)

    bank_step = low_swap(0)
    pair_copies = [
        send(pair_src.at[k], pair_got.at[k], q_ss.at[k], q_rs.at[k], twin) for k in range(NC)
    ]
    bank_step = low_spread(0, bank_step)

    def part(k):
        return send(part_src.at[k], part_got.at[k], p_ss.at[k], p_rs.at[k], c_peers[k])

    part_copies = []
    for k, copy in enumerate(pair_copies):
        copy.wait_recv()
        total = mine[k] + pair_got[k].astype(f32)
        if k == NC - 1:
            acc[...] = total
        else:
            part_src[k] = total.astype(bf16)
            if k < EARLY:
                part_copies.append(part(k))

    loads[6].wait()

    @pl.when(holder)
    def _():
        root_x = index_ref[0] % NX
        for chunk in range(2):

            @pl.when(jnp.logical_not(source))
            def _(chunk=chunk):
                h_copies[chunk][0].wait_recv()

            for copy in x_copies[chunk]:
                copy.start()
        for chunk in range(2):
            arrived(x_copies[chunk])
            y_got[chunk][yh] = x_got[chunk][root_x]
            y_copies[chunk].start()

    part_copies += [part(k) for k in range(EARLY, NC - 1)]
    bank_step = low_join(0, bank_step)

    @pl.when(holder)
    def _():
        root_y = index_ref[0] // (NZ * NX)
        for chunk in range(2):
            y_copies[chunk].wait_recv()
            g_got[chunk][z] = y_got[chunk][root_y]
            for copy in g_copies(chunk, 0, h_peers):
                copy.start()
        for i in range(NL):
            pl.semaphore_wait(ready.at[i], 1)
        for chunk in range(2):
            for copy in g_copies(chunk, NH - 1, late_peers):
                copy.start()

    total = acc[...]
    for k, copy in enumerate(part_copies):
        copy.wait_recv()
        total = total + part_got[k].astype(f32)
    loads[4].wait()
    loads[5].wait()
    acc[...] = total + jnp.where(tenant == 1.0, expanded(0, bank_step, bank_up), 0.0)

    low = None
    for chunk in range(2):
        for h in range(NH):

            @pl.when(z != h)
            def _(chunk=chunk, h=h):
                remote(
                    g_got[chunk].at[h], g_got[chunk].at[h],
                    g_ss.at[chunk, 0], g_rs.at[chunk, h], y_peer,
                ).wait_recv()

            for j in range(WIDE):
                column = chunk * CHUNK + j * HEAD
                value = g_got[chunk][h, 16 * j : 16 * (j + 1), :]
                for row in (16 * h, RANK + 16 * h):
                    ranks[row : row + 16, column : column + HEAD] = value
        columns = slice(chunk * CHUNK, (chunk + 1) * CHUNK)
        term = times_ranks(tok[:, columns], ranks[:, columns])
        low = term if low is None else low + term
    low_start(1, low)
    store_step = low_swap(1)
    for h in range(NH):
        row = 16 * h
        value = g_got[0][h, 16 * WIDE :, :]
        up[row : row + 16, 0:HEAD] = value
        up[RANK + row : RANK + row + 16, HEAD:] = value
    store_step = low_spread(1, store_step)
    store_step = low_join(1, store_step)
    adapted = acc[...] + jnp.where(tenant == 2.0, expanded(1, store_step, up), 0.0)
    swapped = pltpu.roll(adapted, HEAD // 2, 1)
    out_ref[...] = (adapted * cos2[...] + swapped * sin2[...]).astype(bf16)
    for copy in started:
        copy.wait_send()

    @pl.when(source)
    def _():
        for copy in h_copies[0] + h_copies[1]:
            copy.wait_send()

    @pl.when(holder)
    def _():
        for chunk in range(2):
            for copy in x_copies[chunk] + [y_copies[chunk]] + g_copies(chunk, 0, h_peers + late_peers):
                copy.wait_send()


def key_rows(root_z, *args):
    bf16, f32 = jnp.bfloat16, jnp.float32
    vmem = pl.BlockSpec(memory_space=pltpu.VMEM)
    hbm = pl.BlockSpec(memory_space=pl.ANY)
    dma = pltpu.SemaphoreType.DMA

    def slices(n):
        return [pltpu.VMEM((n, 16 * tiles, HEAD), bf16) for tiles in TILES]

    return pl.pallas_call(
        functools.partial(kernel, root_z),
        out_shape=jax.ShapeDtypeStruct((ROWS, HEAD), bf16),
        in_specs=[hbm] * 9,
        out_specs=vmem,
        scratch_shapes=[
            pltpu.SMEM((1,), jnp.int32),
            pltpu.SMEM((1,), jnp.int32),
            pltpu.VMEM((ROWS,), jnp.int32),
            pltpu.VMEM((ROWS, FEAT), bf16),
            pltpu.VMEM((FEAT, 2 * NC * HEAD), bf16),
            pltpu.VMEM((RANK, FEAT), f32),
            pltpu.VMEM((RANK, HEAD), f32),
            pltpu.VMEM((2 * RANK, FEAT), bf16),
            pltpu.VMEM((2 * RANK, FEAT), bf16),
            pltpu.VMEM((2 * RANK, 2 * HEAD), bf16),
            pltpu.VMEM((2 * RANK, 2 * HEAD), bf16),
            *slices(NH), *slices(NX), *slices(NY), *slices(NH),
            pltpu.VMEM((NC, ROWS, HEAD), f32),
            pltpu.VMEM((NC, ROWS, HEAD), bf16),
            pltpu.VMEM((NC, ROWS, HEAD), bf16),
            pltpu.VMEM((NC - 1, ROWS, HEAD), bf16),
            pltpu.VMEM((NC - 1, ROWS, HEAD), bf16),
            pltpu.VMEM((2, PACK, HEAD), f32),
            pltpu.VMEM((2, PACK, HEAD), bf16),
            pltpu.VMEM((2, PACK, HEAD), bf16),
            pltpu.VMEM((2, PACK, HEAD), bf16),
            pltpu.VMEM((2, NC - 1, PACK, HEAD), bf16),
            pltpu.VMEM((2, 2, PACK, HEAD), bf16),
            pltpu.VMEM((ROWS, HEAD), f32),
            pltpu.VMEM((ROWS, HEAD), f32),
            pltpu.VMEM((ROWS, HEAD), f32),
            dma((11,)),
            pltpu.SemaphoreType.REGULAR((NL,)),
            dma((2, NH)), dma((2,)),
            dma((2, NX - 1)), dma((2, NX - 1)),
            dma((2,)), dma((2,)),
            dma((2, NZ - 1)), dma((2, NH)),
            dma((NC,)), dma((NC,)),
            dma((NC - 1,)), dma((NC - 1,)),
            dma((2, NC + 1)), dma((2, NC + 1)),
        ],
        compiler_params=pltpu.CompilerParams(
            collective_id=root_z, has_side_effects=True, vmem_limit_bytes=60 * 1024 * 1024
        ),
        name=f"key_rows_{root_z}",
    )(*args)


def per_device(
    tokens, tenant, offsets, store_index, frozen_key_weight, store_a, store_b, bank_a, bank_b
):
    return lax.switch(
        lax.rem(lax.div(store_index[0], NX), NZ),
        [functools.partial(key_rows, z) for z in range(NZ)],
        store_index,
        offsets,
        tenant,
        tokens,
        frozen_key_weight,
        store_a[0],
        store_b[0].T,
        bank_a,
        bank_b.T,
    )


def solution(mesh):
    in_specs = (
        P("rep", "tp"),
        P("rep"),
        P("rep"),
        P(),
        P("tp", None),
        P("rep", None, "tp"),
        P("rep", "tp", None),
        P(None, "tp"),
        P("tp", None),
    )
    return jax.shard_map(
        per_device, mesh=mesh, in_specs=in_specs, out_specs=P("rep", "tp"), check_vma=False
    )
```

```python
import functools
import math

import jax
import jax.numpy as jnp
from jax import lax
from jax.experimental import pallas as pl
from jax.experimental.pallas import tpu as pltpu
from jax.sharding import PartitionSpec as P

MESH = pl.DeviceIdType.MESH
SCALE = 2.0
NY, NZ, NX = 2, 8, 4
NC = 4
ROWS = 384
FEAT = 1536
HEAD = 128
RANK = 64
HALF = ROWS // 2
PACK = ROWS // 4
NH = 4
NL = NZ - NH
EARLY = 1
WIDE = 6
TILES = (WIDE + 1, WIDE)
CHUNK = FEAT // 2


def kernel(
    root_y, pair,
    index_hbm, offset_hbm, tenant_hbm, tok_hbm, w_hbm, a_hbm, bt_hbm, ba_hbm, bbt_hbm, out_ref,
    index_ref, offset_ref, tenant_ref, tok, w, a_raw, bt_raw, bank, ranks, bank_up, up,
    src0, src1, s_got0, s_got1, x_got0, x_got1, g_got0, g_got1,
    mine, pair_src, pair_got, part_src, part_got,
    l_mine, l_src, l_got, l_chip, l_chips, l_all,
    acc, cos2, sin2,
    load_sem, ready,
    h_ss, h_rs, x_ss, x_rs, y_ss, y_rs, g_ss, g_rs, q_ss, q_rs, p_ss, p_rs, l_ss, l_rs,
):
    bf16, f32 = jnp.bfloat16, jnp.float32
    rep, t = lax.axis_index("rep"), lax.axis_index("tp")
    yh, z, x = rep // (NZ * NX), (rep // NX) % NZ, rep % NX
    yl, core = t // 2, t % 2

    def at(yh_, z_, x_):
        return (yh_ * NZ + z_) * NX + x_

    x_of = [(x + k) % NX for k in range(1, NX)]
    c_of = [(yl + k) % NC for k in range(1, NC)]
    holder = z < NH
    home, source = holder & (yh == root_y), (z // 2 == pair) & (yh == root_y)
    low_z = 2 * pair
    h_of = [(z + k) % NH for k in range(1, NH)]
    h_peers = [(at(yh, q, x), t) for q in h_of]
    holders = [(at(yh, q, x), t) for q in range(NH)]
    late_peers = [(at(yh, NH + q, x), t) for q in range(NL)]
    x_peers = [(at(yh, z, q), t) for q in x_of]
    y_peer = (at(1 - yh, z, x), t)
    c_peers = [(rep, 2 * q + core) for q in c_of]
    twin = (rep, 2 * yl + 1 - core)

    barrier = pltpu.get_barrier_semaphore()

    def greet(peers):
        for peer in peers:
            pl.semaphore_signal(barrier, inc=1, device_id=peer, device_id_type=MESH)

    greet(c_peers + [twin])

    @pl.when(holder)
    def _():
        greet(h_peers + x_peers + [y_peer] + late_peers)

    bank_up[...] = jnp.zeros_like(bank_up)
    up[...] = jnp.zeros_like(up)
    loads = [
        pltpu.make_async_copy(src, dst, load_sem.at[i])
        for i, (src, dst) in enumerate(
            [
                (tok_hbm, tok),
                (ba_hbm, bank.at[pl.ds(0, RANK)]),
                (ba_hbm, bank.at[pl.ds(RANK, RANK)]),
                (w_hbm, w),
                (bbt_hbm, bank_up.at[pl.ds(0, RANK), pl.ds(0, HEAD)]),
                (bbt_hbm, bank_up.at[pl.ds(RANK, RANK), pl.ds(HEAD, HEAD)]),
                (index_hbm, index_ref),
                (offset_hbm, offset_ref),
                (tenant_hbm, tenant_ref),
                (a_hbm, a_raw),
                (bt_hbm, bt_raw),
            ]
        )
    ]

    @pl.when(source)
    def _():
        for load in loads[9:]:
            load.start()

    for load in loads[:9]:
        load.start()

    src, s_got, x_got, g_got = (
        (src0, src1), (s_got0, s_got1), (x_got0, x_got1), (g_got0, g_got1)
    )

    started = []

    def remote(src, dst, ss, rs, peer):
        return pltpu.make_async_remote_copy(
            src_ref=src, dst_ref=dst, send_sem=ss, recv_sem=rs, device_id=peer, device_id_type=MESH
        )

    def send(*args):
        copy = remote(*args)
        copy.start()
        started.append(copy)
        return copy

    def arrived(copies):
        for copy in copies:
            copy.wait_recv()

    far = list(zip(h_of, h_peers)) if low_z < NH else list(enumerate(holders))
    h_copies = [
        [
            remote(
                src[chunk].at[h], s_got[chunk].at[z % 2],
                h_ss.at[chunk, i], h_rs.at[chunk, z % 2], peer,
            )
            for i, (h, peer) in enumerate(far)
        ]
        for chunk in range(2)
    ]
    x_copies = [
        [
            remote(
                x_got[chunk].at[x], x_got[chunk].at[x],
                x_ss.at[chunk, i], x_rs.at[chunk, i], x_peers[i],
            )
            for i in range(NX - 1)
        ]
        for chunk in range(2)
    ]
    y_copies = [
        remote(g_got[chunk].at[z], g_got[chunk].at[z], y_ss.at[chunk], y_rs.at[chunk], y_peer)
        for chunk in range(2)
    ]

    def g_copies(chunk, first, peers):
        return [
            remote(
                g_got[chunk].at[z], g_got[chunk].at[z],
                g_ss.at[chunk, first + i], g_rs.at[chunk, z], peer,
            )
            for i, peer in enumerate(peers)
        ]

    lane = lax.broadcasted_iota(jnp.int32, (PACK, HEAD), 1)
    left = lane < RANK

    def low_start(s, low):
        halves = [
            jnp.where(left, low[HALF * h : HALF * h + PACK], low[HALF * h + PACK : HALF * (h + 1)])
            for h in range(2)
        ]
        l_mine[s] = jnp.where(core == 0, halves[0], halves[1])
        l_src[s] = jnp.where(core == 0, halves[1], halves[0]).astype(bf16)

    def low_swap(s):
        return send(l_src.at[s], l_got.at[s], l_ss.at[s, 0], l_rs.at[s, 0], twin)

    def low_spread(s, copy):
        copy.wait_recv()
        l_chip[s] = (l_mine[s] + l_got[s].astype(f32)).astype(bf16)
        return [
            send(l_chip.at[s], l_chips.at[s, i], l_ss.at[s, 1 + i], l_rs.at[s, 1 + i], c_peers[i])
            for i in range(NC - 1)
        ]

    def low_join(s, copies):
        total = l_chip[s].astype(f32)
        for i, copy in enumerate(copies):
            copy.wait_recv()
            total = total + l_chips[s, i].astype(f32)
        l_all[s, core] = total.astype(bf16)
        return send(l_all.at[s, core], l_all.at[s, core], l_ss.at[s, NC], l_rs.at[s, NC], twin)

    def expanded(s, copy, ups):
        copy.wait_recv()
        parts = []
        for h in range(2):
            both = jnp.dot(l_all[s, h], ups[...], preferred_element_type=f32)
            parts += [both[:, :HEAD], both[:, HEAD:]]
        return SCALE * jnp.concatenate(parts, axis=0)

    def times_ranks(a, b):
        return lax.dot_general(a, b, (((1,), (1,)), ((), ())), preferred_element_type=f32)

    def greeted():
        replica = NC
        pl.semaphore_wait(barrier, replica + jnp.where(holder, NH + NX - 1, NH))

    def cut():
        for load in loads[9:]:
            load.wait()
        for chunk in range(2):
            for h in range(NH):
                for j in range(WIDE):
                    column = chunk * CHUNK + j * HEAD
                    src[chunk][h, 16 * j : 16 * (j + 1), :] = a_raw[
                        16 * h : 16 * (h + 1), column : column + HEAD
                    ].astype(bf16)
                if chunk == 0:
                    src[chunk][h, 16 * WIDE :, :] = bt_raw[16 * h : 16 * (h + 1), :].astype(bf16)
            if low_z < NH:
                s_got[chunk][z % 2] = src[chunk][z]

    def push():
        for chunk in range(2):
            for copy in h_copies[chunk]:
                copy.start()

    source_first = low_z >= NH
    if source_first:

        @pl.when(source)
        def _():
            cut()
            greeted()
            push()

    loads[0].wait()
    loads[1].wait()
    loads[2].wait()
    low_start(0, times_ranks(tok[...], bank[...]))
    loads[3].wait()
    order = c_of + [yl]
    for k, q in enumerate(order):
        column = pl.multiple_of(q * 2 * HEAD, 2 * HEAD)
        both = jnp.dot(tok[...], w[:, pl.ds(column, 2 * HEAD)], preferred_element_type=f32)
        mine[k] = jnp.where(core == 0, both[:, :HEAD], both[:, HEAD:])
        pair_src[k] = jnp.where(core == 0, both[:, HEAD:], both[:, :HEAD]).astype(bf16)

    loads[7].wait()
    wide = lax.broadcasted_iota(jnp.int32, (HALF, HEAD), 1)
    row = lax.broadcasted_iota(jnp.int32, (HALF, HEAD), 0)
    row = jnp.where(wide < HEAD // 2, row, row + HALF)
    freq = jnp.exp((wide % (HEAD // 2)).astype(f32) * (-2.0 * math.log(1000000.0) / HEAD))
    angle = (offset_ref[0] + row).astype(f32) * freq
    first = wide < HEAD // 2
    cosine, sine = jnp.cos(angle), jnp.sin(angle)
    turned_cos, turned_sin = pltpu.roll(cosine, HEAD // 2, 1), pltpu.roll(sine, HEAD // 2, 1)
    cos2[0:HALF, :] = jnp.where(first, cosine, turned_cos)
    cos2[HALF:, :] = jnp.where(first, turned_cos, cosine)
    sin2[0:HALF, :] = jnp.where(first, -sine, turned_sin)
    sin2[HALF:, :] = jnp.where(first, -turned_sin, sine)

    loads[8].wait()
    eye = lax.broadcasted_iota(jnp.int32, (HEAD, HEAD), 0) == lax.broadcasted_iota(
        jnp.int32, (HEAD, HEAD), 1
    )
    tenant = jnp.concatenate(
        [
            jnp.sum(
                jnp.where(eye, tenant_ref[pl.ds(HEAD * i, HEAD)].reshape(1, HEAD), 0).astype(f32),
                axis=1,
                keepdims=True,
            )
            for i in range(ROWS // HEAD)
        ],
        axis=0,
    )

    if source_first:

        @pl.when(jnp.logical_not(source))
        def _():
            greeted()
    else:

        @pl.when(source)
        def _():
            cut()

        greeted()

        @pl.when(source)
        def _():
            push()

    @pl.when(jnp.logical_not(holder))
    def _():
        for peer in holders:
            pl.semaphore_signal(ready.at[z - NH], inc=1, device_id=peer, device_id_type=MESH)

    bank_step = low_swap(0)
    pair_copies = [
        send(pair_src.at[k], pair_got.at[k], q_ss.at[k], q_rs.at[k], twin) for k in range(NC)
    ]
    bank_step = low_spread(0, bank_step)

    def part(k):
        return send(part_src.at[k], part_got.at[k], p_ss.at[k], p_rs.at[k], c_peers[k])

    part_copies = []
    for k, copy in enumerate(pair_copies):
        copy.wait_recv()
        total = mine[k] + pair_got[k].astype(f32)
        if k == NC - 1:
            acc[...] = total
        else:
            part_src[k] = total.astype(bf16)
            if k < EARLY:
                part_copies.append(part(k))

    loads[6].wait()

    @pl.when(home)
    def _():
        root_x, root_z = index_ref[0] % NX, (index_ref[0] // NX) % NZ
        for chunk in range(2):
            for i in range(2):

                @pl.when(z != low_z + i)
                def _(chunk=chunk, i=i):
                    remote(
                        s_got[chunk].at[i], s_got[chunk].at[i],
                        h_ss.at[chunk, 0], h_rs.at[chunk, i], y_peer,
                    ).wait_recv()

            x_got[chunk][x] = s_got[chunk][root_z % 2]
            for copy in x_copies[chunk]:
                copy.start()
        for chunk in range(2):
            arrived(x_copies[chunk])
            g_got[chunk][z] = x_got[chunk][root_x]
            y_copies[chunk].start()
            for copy in g_copies(chunk, 0, h_peers):
                copy.start()

    part_copies += [part(k) for k in range(EARLY, NC - 1)]
    bank_step = low_join(0, bank_step)

    @pl.when(holder & jnp.logical_not(home))
    def _():
        for chunk in range(2):
            y_copies[chunk].wait_recv()
            for copy in g_copies(chunk, 0, h_peers):
                copy.start()

    @pl.when(holder)
    def _():
        for i in range(NL):
            pl.semaphore_wait(ready.at[i], 1)
        for chunk in range(2):
            for copy in g_copies(chunk, NH - 1, late_peers):
                copy.start()

    low = None
    for chunk in range(2):
        for h in range(NH):

            @pl.when(z != h)
            def _(chunk=chunk, h=h):
                remote(
                    g_got[chunk].at[h], g_got[chunk].at[h],
                    g_ss.at[chunk, 0], g_rs.at[chunk, h], y_peer,
                ).wait_recv()

            for j in range(WIDE):
                column = chunk * CHUNK + j * HEAD
                value = g_got[chunk][h, 16 * j : 16 * (j + 1), :]
                for row in (16 * h, RANK + 16 * h):
                    ranks[row : row + 16, column : column + HEAD] = value
        columns = slice(chunk * CHUNK, (chunk + 1) * CHUNK)
        term = times_ranks(tok[:, columns], ranks[:, columns])
        low = term if low is None else low + term
    low_start(1, low)
    store_step = low_swap(1)
    for h in range(NH):
        row = 16 * h
        value = g_got[0][h, 16 * WIDE :, :]
        up[row : row + 16, 0:HEAD] = value
        up[RANK + row : RANK + row + 16, HEAD:] = value
    store_step = low_spread(1, store_step)

    total = acc[...]
    for k, copy in enumerate(part_copies):
        copy.wait_recv()
        total = total + part_got[k].astype(f32)
    loads[4].wait()
    loads[5].wait()
    acc[...] = total + jnp.where(tenant == 1.0, expanded(0, bank_step, bank_up), 0.0)

    store_step = low_join(1, store_step)
    adapted = acc[...] + jnp.where(tenant == 2.0, expanded(1, store_step, up), 0.0)
    swapped = pltpu.roll(adapted, HEAD // 2, 1)
    out_ref[...] = (adapted * cos2[...] + swapped * sin2[...]).astype(bf16)
    for copy in started:
        copy.wait_send()

    @pl.when(source)
    def _():
        for copy in h_copies[0] + h_copies[1]:
            copy.wait_send()

    @pl.when(holder)
    def _():
        for chunk in range(2):
            for copy in g_copies(chunk, 0, h_peers + late_peers):
                copy.wait_send()

    @pl.when(home)
    def _():
        for chunk in range(2):
            for copy in x_copies[chunk] + [y_copies[chunk]]:
                copy.wait_send()


def key_rows(root_y, pair, *args):
    bf16, f32 = jnp.bfloat16, jnp.float32
    vmem = pl.BlockSpec(memory_space=pltpu.VMEM)
    hbm = pl.BlockSpec(memory_space=pl.ANY)
    dma = pltpu.SemaphoreType.DMA

    def slices(n):
        return [pltpu.VMEM((n, 16 * tiles, HEAD), bf16) for tiles in TILES]

    return pl.pallas_call(
        functools.partial(kernel, root_y, pair),
        out_shape=jax.ShapeDtypeStruct((ROWS, HEAD), bf16),
        in_specs=[hbm] * 9,
        out_specs=vmem,
        scratch_shapes=[
            pltpu.SMEM((1,), jnp.int32),
            pltpu.SMEM((1,), jnp.int32),
            pltpu.VMEM((ROWS,), jnp.int32),
            pltpu.VMEM((ROWS, FEAT), bf16),
            pltpu.VMEM((FEAT, 2 * NC * HEAD), bf16),
            pltpu.VMEM((RANK, FEAT), f32),
            pltpu.VMEM((RANK, HEAD), f32),
            pltpu.VMEM((2 * RANK, FEAT), bf16),
            pltpu.VMEM((2 * RANK, FEAT), bf16),
            pltpu.VMEM((2 * RANK, 2 * HEAD), bf16),
            pltpu.VMEM((2 * RANK, 2 * HEAD), bf16),
            *slices(NH), *slices(2), *slices(NX), *slices(NH),
            pltpu.VMEM((NC, ROWS, HEAD), f32),
            pltpu.VMEM((NC, ROWS, HEAD), bf16),
            pltpu.VMEM((NC, ROWS, HEAD), bf16),
            pltpu.VMEM((NC - 1, ROWS, HEAD), bf16),
            pltpu.VMEM((NC - 1, ROWS, HEAD), bf16),
            pltpu.VMEM((2, PACK, HEAD), f32),
            pltpu.VMEM((2, PACK, HEAD), bf16),
            pltpu.VMEM((2, PACK, HEAD), bf16),
            pltpu.VMEM((2, PACK, HEAD), bf16),
            pltpu.VMEM((2, NC - 1, PACK, HEAD), bf16),
            pltpu.VMEM((2, 2, PACK, HEAD), bf16),
            pltpu.VMEM((ROWS, HEAD), f32),
            pltpu.VMEM((ROWS, HEAD), f32),
            pltpu.VMEM((ROWS, HEAD), f32),
            dma((11,)),
            pltpu.SemaphoreType.REGULAR((NL,)),
            dma((2, NH)), dma((2, 2)),
            dma((2, NX - 1)), dma((2, NX - 1)),
            dma((2,)), dma((2,)),
            dma((2, NZ - 1)), dma((2, NH)),
            dma((NC,)), dma((NC,)),
            dma((NC - 1,)), dma((NC - 1,)),
            dma((2, NC + 1)), dma((2, NC + 1)),
        ],
        compiler_params=pltpu.CompilerParams(
            collective_id=root_y * (NZ // 2) + pair, has_side_effects=True, vmem_limit_bytes=60 * 1024 * 1024
        ),
        name=f"key_rows_{root_y}_{pair}",
    )(*args)


def per_device(
    tokens, tenant, offsets, store_index, frozen_key_weight, store_a, store_b, bank_a, bank_b
):
    return lax.switch(
        lax.div(store_index[0], 2 * NX),
        [functools.partial(key_rows, y, p) for y in range(NY) for p in range(NZ // 2)],
        store_index,
        offsets,
        tenant,
        tokens,
        frozen_key_weight,
        store_a[0],
        store_b[0].T,
        bank_a,
        bank_b.T,
    )


def solution(mesh):
    in_specs = (
        P("rep", "tp"),
        P("rep"),
        P("rep"),
        P(),
        P("tp", None),
        P("rep", None, "tp"),
        P("rep", "tp", None),
        P(None, "tp"),
        P("tp", None),
    )
    return jax.shard_map(
        per_device, mesh=mesh, in_specs=in_specs, out_specs=P("rep", "tp"), check_vma=False
    )
```
